128 devices in a mesh: gx: 8 (over z, core), gy: 16 (over y, x).
Axes of the slice: x: 4, y: 4, z: 4, core: 2. Of those that a mesh axis runs over, the one named last changes fastest.
Arguments:
- canopy: float32 [8, 64, 128, 1024], P(None, None, 'gy', 'gx'), may hold values from -6 to 6
- courant: float32 [2, 64], replicated, may hold values from -0.35 to 0.35
- walls: float32 [6, 128, 32768], P(None, None, ('gx', 'gy')), may hold values from -6 to 6
- inverses: float32 [8, 128, 128], replicated, as said below
- package: int32 [32768], P(('gx', 'gy')), may hold values from 0 to 7
- surf_coeff: float32 [6, 32768], P(None, ('gx', 'gy')), may hold values from 0.2 to 2
- facade_area: float32 [64, 32768], P(None, ('gx', 'gy')), may hold values from 0.05 to 1
- anchor: int32 [32768, 1], P(('gx', 'gy')), may hold values from 0 to 127; in each aligned block of 256 rows (0 to 255, 256 to 511, ...) at most 10 rows name the same one
- footprint: int32 [32768, 8], P(('gx', 'gy')), may hold values from 0 to 1023
Outputs:
- canopy_out: float32 [8, 64, 128, 1024], P(None, None, 'gy', 'gx')
- building_air: float32 [2, 64, 32768], P(None, None, ('gx', 'gy'))
- walls_out: float32 [6, 128, 32768], P(None, None, ('gx', 'gy'))
The draws below stay inside these ranges and needn't reach their ends.
Inputs may be any that keep to these rules, and one draw needn't show every extreme that they name: The footprint of building b lies in the tile of the device with linear index anchor[b, 0] over gx and gy, gx slowest; among the 256 buildings of one device at most 10 share an anchor. `footprint`: a cell y * 128 + x with y, x local to the anchor tile. `inverses`: one matrix per retrofit package.
All inputs are finite; a program needn't handle non-finite values.
Results may differ from the reference program's by a relative error of at most 0.0003.
Values sent between devices are 32-bit elements; how exact they have to be, the bound alone decides.
No kernel may reach another device: no remote copies, remote signals or barrier semaphores. Data moves between devices by JAX's collectives and lax.ppermute only.
A program may use at most 128 MiB of HBM per device.

```python
import math
import jax
import jax.numpy as jnp
import numpy as np
from jax import lax

F = 8
LEV = 64
CX = 128
CY = 8
NODES = 128
SURF = 6
PKG = 8
FOOT = 8
SUB = 4
BLD_DEV = 256
CAP = 10
BUILDINGS = 32768
NX = 1024
NY = 128
N_GY = 16
DEVICES = 128


def draw_inverses(key, part):
    first_key, second_key = jax.random.split(jax.random.fold_in(key, 11))
    diagonal = jax.random.uniform(first_key, (PKG, NODES), jnp.float32, 0.4, 0.7)
    offdiag = 0.02 * jax.random.normal(second_key, (PKG, NODES, NODES), jnp.float32)
    identity = jnp.eye(NODES, dtype=jnp.float32)
    return offdiag * (1.0 - identity)[None] + diagonal[:, :, None] * identity[None]


def plant(values, rng, low, high):
    shape = values.shape
    index_at = [jax.random.randint(jax.random.fold_in(rng, axis), (), 0, shape[axis]) for axis in range(len(shape))]
    values = values.at[tuple(index_at)].set(low)
    longest = shape.index(max(shape))
    index_at[longest] = (index_at[longest] + 1) % shape[longest]
    return values.at[tuple(index_at)].set(high)


def block_scale(stream_key, shape, cuts, least, top_value):
    factor_of = 1.0
    for dim, parts in cuts:
        draws = jax.random.uniform(jax.random.fold_in(jax.random.fold_in(stream_key, 6), dim), (parts,), jnp.float32, least / len(cuts), top_value / len(cuts))
        factor_of = factor_of * jnp.repeat(jnp.exp(draws), shape[dim] // parts).reshape((-1,) + (1,) * (len(shape) - 1 - dim))
    return factor_of


def shared_out(rng, own, number, rows, count, top, most, lean):
    sequence = jax.random.permutation(rng, count)
    heavy_load, common = portions_of(count, rows * top, most, lean, True), portions_of(count, rows * top, most, lean, False)
    places = jnp.arange(count)

    def named(lengths, rotation):
        used = int((lengths > 0).sum())
        fixed = max(1, used // 4)
        moved = fixed + (places - fixed + rotation * (used - fixed)) % max(1, count - fixed)
        return jnp.zeros((count,), jnp.int32).at[sequence[jnp.where(places < fixed, places, moved)]].set(jnp.asarray(lengths, jnp.int32))

    lengths = jnp.where(number % 4 == 0, named(heavy_load, number // 4), named(common, number - number // 4 - 1))
    mixed = jax.random.permutation(jax.random.fold_in(own, 3), count)
    giver, receiver = mixed[0:count // 2 * 2:2], mixed[1:count // 2 * 2:2]
    slack = jnp.minimum(lengths[giver] - 1, most - lengths[receiver]) // 2
    slack = jnp.where((giver == sequence[0]) | (receiver == sequence[0]) | (lengths[receiver] == 0), 0, jnp.maximum(slack, 0))
    moved = jax.random.randint(jax.random.fold_in(own, 4), (count // 2,), 0, 1 << 20) % (slack + 1)
    lengths = lengths.at[giver].add(-moved).at[receiver].add(moved)
    items = jnp.searchsorted(jnp.cumsum(lengths), jnp.arange(rows * top), side="right").astype(jnp.int32)
    listing = items.reshape(top, rows).T
    listing = listing[jax.random.permutation(jax.random.fold_in(own, 1), rows)]
    rotation = jax.random.randint(jax.random.fold_in(own, 2), (rows, 1), 0, top)
    return jnp.take_along_axis(listing, (jnp.arange(top)[None, :] + rotation) % top, axis=1)


def portions_of(amount, total, reach, lean, full):
    weights = [(1 << 20) // math.isqrt(rank ** lean) + 1 for rank in range(1, amount + 1)]
    largest = reach if full else min(reach, max(-(-total // amount), total * weights[0] // sum(weights)))
    least = 1 if total - largest >= amount - 1 else 0
    holding, rest = [largest] + [least] * (amount - 1), total - largest - least * (amount - 1)
    while rest > 0:
        candidates = [i for i in range(1, amount) if holding[i] < largest] or [i for i in range(1, amount) if holding[i] < reach]
        mass, remaining = sum([weights[i] for i in candidates]), rest
        for i in candidates:
            more = min(reach - holding[i], max(1, remaining * weights[i] // mass), rest)
            holding[i] = holding[i] + more
            rest = rest - more
    return np.array(holding)


def normal_values(rng, dims, deviation, reach, shards=(), held_as=jnp.bfloat16):
    values = jax.random.normal(rng, dims, jnp.float32) * deviation
    if len(shards) > 0:
        values = block_scale(rng, dims, shards, -0.22, 0.18) * values
    return jnp.clip(values, min=-reach, max=reach).astype(held_as)


def setup_inputs(seed: int = 0) -> dict:
    arg_keys = jax.random.split(jax.random.key(seed), 10)
    canopy = normal_values(arg_keys[0], (F, LEV, NY, NX), 1.0, 6.0, ((2, 16), (3, 8)), jnp.float32)
    courant = jnp.clip(jax.random.uniform(arg_keys[1], (2, LEV), jnp.float32, -0.35, 0.35), -0.35, 0.35)
    walls = normal_values(arg_keys[2], (SURF, NODES, BUILDINGS), 1.0, 6.0, ((2, 128),), jnp.float32)
    inverses = draw_inverses(jax.random.fold_in(arg_keys[9], 71), 0)
    package = plant(jax.random.randint(arg_keys[4], (BUILDINGS,), 0, PKG), jax.random.fold_in(arg_keys[4], 1), 0, PKG - 1).astype(jnp.int32)
    surf_coeff = jnp.clip(jnp.exp(math.log(2.0) - 2.3025851 * jax.random.uniform(arg_keys[5], (SURF, BUILDINGS), jnp.float32) ** block_scale(arg_keys[5], (SURF, BUILDINGS), ((1, 128),), -0.2, 0.2)), 0.2, 2.0)
    facade_area = jnp.clip(jnp.exp(math.log(1.0) - 2.9957323 * jax.random.uniform(arg_keys[6], (LEV, BUILDINGS), jnp.float32) ** block_scale(arg_keys[6], (LEV, BUILDINGS), ((1, 128),), -0.2, 0.2)), 0.05, 1.0)
    anchor_keys = jax.random.split(jax.random.fold_in(arg_keys[7], 1), BUILDINGS // BLD_DEV)
    anchor_turns = jax.random.permutation(jax.random.fold_in(arg_keys[7], 3), BUILDINGS // BLD_DEV)
    anchor = jax.vmap(lambda own, number: shared_out(jax.random.fold_in(arg_keys[7], 2), own, number, BLD_DEV, DEVICES, 1, CAP, 2))(anchor_keys, anchor_turns).reshape((BUILDINGS, 1))
    footprint = plant(jax.random.randint(arg_keys[8], (BUILDINGS, FOOT), 0, CX * CY), jax.random.fold_in(arg_keys[8], 1), 0, (CX * CY) - 1).astype(jnp.int32)
    return {"canopy": canopy, "courant": courant, "walls": walls, "inverses": inverses, "package": package, "surf_coeff": surf_coeff, "facade_area": facade_area, "anchor": anchor, "footprint": footprint}


source_rate = 0.1
kappa_rate = 0.05
vertical_rate = 0.05
wall_gain = 0.5


def stencil(padded, courant):
    center = padded[..., 1:-1, 1:-1]
    west_cells = padded[..., 1:-1, :-2]
    east_cells = padded[..., 1:-1, 2:]
    south_cells = padded[..., :-2, 1:-1]
    north_cells = padded[..., 2:, 1:-1]
    courant_x = courant[0][:, None, None]
    courant_y = courant[1][:, None, None]
    upwind = jnp.maximum(courant_x, 0.0) * (center - west_cells) + jnp.minimum(courant_x, 0.0) * (east_cells - center)
    upwind = upwind + jnp.maximum(courant_y, 0.0) * (center - south_cells) + jnp.minimum(courant_y, 0.0) * (north_cells - center)
    spread = east_cells + west_cells + north_cells + south_cells - 4.0 * center
    above = jnp.concatenate([center[..., 1:, :, :], center[..., -1:, :, :]], axis=-3)
    below = jnp.concatenate([center[..., :1, :, :], center[..., :-1, :, :]], axis=-3)
    vertical = above + below - 2.0 * center
    return center - upwind + kappa_rate * spread + vertical_rate * vertical


def select_walls(inverses, rhs_walls, package):
    result = jnp.zeros_like(rhs_walls)
    for package_id in range(PKG):
        product = jnp.einsum("nm,smb->snb", inverses[package_id], rhs_walls, precision=lax.Precision.HIGHEST)
        result = jnp.where((package == package_id)[None, None, :], product, result)
    return result


def reference(canopy, courant, walls, inverses, package, surf_coeff, facade_area, anchor, footprint):
    surface = walls[:, 0, :]
    heat = jnp.sum(surf_coeff * surface, axis=0)
    coupling = jnp.sum(surf_coeff, axis=0)
    payload = jnp.concatenate([facade_area * heat[None, :], facade_area * coupling[None, :]], axis=0).T
    target = anchor[:, 0]
    y_base = (target % N_GY) * CY
    x_base = (target // N_GY) * CX
    global_cell = ((y_base[:, None] + footprint // CX) * NX + x_base[:, None] + footprint % CX).astype(jnp.int32)
    summed = jnp.zeros((NY * NX, 2 * LEV), jnp.float32)
    for foot_id in range(FOOT):
        summed = summed.at[global_cell[:, foot_id]].add(payload)
    psum = summed[:, :LEV].T.reshape(LEV, NY, NX)
    qsum = summed[:, LEV:].T.reshape(LEV, NY, NX)
    theta = canopy.at[0].add(source_rate * (psum - qsum * canopy[0]) / FOOT)

    def advance(field):
        for step in range(SUB):
            padded = jnp.pad(field, ((0, 0), (1, 1), (1, 1)))
            field = stencil(padded, courant)
        return field

    canopy_out = lax.map(advance, theta)
    flat_theta = canopy_out[:2].reshape(2, LEV, NY * NX)
    air_sum = jnp.zeros((2, LEV, BUILDINGS), jnp.float32)
    for foot_id in range(FOOT):
        air_sum = air_sum + flat_theta[:, :, global_cell[:, foot_id]]
    building_air = air_sum / FOOT
    air_temp = jnp.sum(facade_area * building_air[0], axis=0) / jnp.sum(facade_area, axis=0)
    wall_source = wall_gain * surf_coeff * (air_temp[None, :] - surface)
    rhs_walls = walls.at[:, 0, :].add(wall_source)
    wall_blocks = jnp.moveaxis(rhs_walls.reshape(SURF, NODES, DEVICES, BLD_DEV), 2, 0)
    package_blocks = package.reshape(DEVICES, BLD_DEV)

    def conduct(pair):
        return select_walls(inverses, pair[0], pair[1])

    solved = lax.map(conduct, (wall_blocks, package_blocks))
    walls_out = jnp.moveaxis(solved, 0, 2).reshape(SURF, NODES, BUILDINGS)
    return canopy_out, building_air, walls_out
```

```python
import functools

import jax
import jax.numpy as jnp
from jax import lax
from jax.experimental import pallas as pl
from jax.experimental.pallas import tpu as pltpu
from jax.sharding import PartitionSpec as P

PKG = 8
SUB = 4
HALO = 4
CAP = 10
FOOT = 8
DEV = 128
LEV = 64
NB = 256
ROWS_Y = 8
LANES = 128
FLUX_ROWS = 6
STRIP = 8
AUX = 2 + FOOT
EARLY = 1

source_rate = 0.1
kappa_rate = 0.05
vertical_rate = 0.05
wall_gain = 0.5

f32 = jnp.float32
bf16 = jnp.bfloat16
VMEM = 32 * 1024 * 1024
NT = (((1,), (1,)), ((), ()))
NN = (((1,), (0,)), ((), ()))


def params(**kw):
    return pltpu.CompilerParams(vmem_limit_bytes=VMEM, **kw)


def whole(shape):
    return pl.BlockSpec(shape, lambda *_: (0,) * len(shape))


def halves(x):
    hi = x.astype(bf16)
    lo = (x - hi.astype(f32)).astype(bf16)
    return hi, lo


def mm(a, b, dims):
    return lax.dot_general(a, b, dims, preferred_element_type=f32)


def payload_kernel(anchor, foot, coeff, walls, facade, out, code_out, aux):
    owner = lax.broadcasted_iota(jnp.int32, (DEV, NB), 0) == anchor[...]
    earlier = lax.broadcasted_iota(jnp.int32, (NB, NB), 0) < lax.broadcasted_iota(
        jnp.int32, (NB, NB), 1
    )
    rank = mm(jnp.where(owner, 1.0, 0.0).astype(bf16), jnp.where(earlier, 1.0, 0.0).astype(bf16), NN)
    code = jnp.where(owner, rank, -1.0)
    code_out[...] = code
    heat = jnp.sum(coeff[...] * walls[:, 0, :], axis=0, keepdims=True)
    coupling = jnp.sum(coeff[...], axis=0, keepdims=True)
    cells = foot[...].astype(f32)
    picks = [jnp.where(code == float(r), 1.0, 0.0).astype(bf16) for r in range(CAP)]
    hi, lo = halves(facade[...])
    zero = jnp.zeros((LEV, NB), bf16)
    even = jnp.concatenate([picks[2 * p] for p in range(CAP // 2)], axis=0)
    odd = jnp.concatenate([picks[2 * p + 1] for p in range(CAP // 2)], axis=0)
    rows = (
        mm(even, jnp.concatenate([hi, zero], axis=0), NT)
        + mm(odd, jnp.concatenate([zero, hi], axis=0), NT)
        + mm(even, jnp.concatenate([lo, zero], axis=0), NT)
        + mm(odd, jnp.concatenate([zero, lo], axis=0), NT)
    )
    for p in range(CAP // 2):
        out[pl.ds(p, DEV, stride=FLUX_ROWS), :] = rows[p * DEV : (p + 1) * DEV]
    aux[...] = jnp.zeros_like(aux)
    for r in range(CAP):
        aux[r, AUX * r : AUX * r + 1, :] = heat
        aux[r, AUX * r + 1 : AUX * r + 2, :] = coupling
        aux[r, AUX * r + 2 : AUX * r + AUX, :] = cells
    total = jnp.zeros((DEV, LANES), f32)
    for r in range(CAP):
        hi, lo = halves(aux[r])
        total = total + mm(picks[r], hi, NT) + mm(picks[r], lo, NT)
    out[pl.ds(CAP // 2, DEV, stride=FLUX_ROWS), :] = total


def payload(anchor, foot, coeff, walls, facade):
    return pl.pallas_call(
        payload_kernel,
        grid=(1,),
        in_specs=[
            whole((1, NB)),
            whole((FOOT, NB)),
            whole((6, NB)),
            pl.BlockSpec((6, 8, NB), lambda _: (0, 0, 0)),
            whole((LEV, NB)),
        ],
        out_specs=[whole((DEV * FLUX_ROWS, LANES)), whole((DEV, NB))],
        out_shape=[
            jax.ShapeDtypeStruct((DEV * FLUX_ROWS, LANES), f32),
            jax.ShapeDtypeStruct((DEV, NB), f32),
        ],
        scratch_shapes=[pltpu.VMEM((CAP, LANES, NB), f32)],
        compiler_params=params(),
        name="payload",
    )(anchor, foot, coeff, walls, facade)


def lane_slot():
    return lax.broadcasted_iota(jnp.int32, (8, LANES), 1)


def pack_row(blocks):
    lane = lane_slot()
    slot = lane % 16
    out = jnp.zeros((8, LANES), f32)
    for i, block in enumerate(blocks):
        here = lane // 16 == i
        west = here & (slot >= 4) & (slot < 8)
        east = here & (slot >= 8) & (slot < 12)
        out = jnp.where(west, pltpu.roll(block, (16 * i + 4) % LANES, 1), out)
        out = jnp.where(east, pltpu.roll(block, (16 * i + 12) % LANES, 1), out)
    return out


def emit_row(y, field, low, high, pack):
    dst = low if y < HALO else high
    dst[0, y % HALO, :, :] = field
    pack[0, y] = pack_row([field[8 * i : 8 * i + 8] for i in range(8)])


def prep_kernel(canopy, low, high, pack):
    for y in range(ROWS_Y):
        emit_row(y, canopy[0, pl.ds(y, LEV, stride=ROWS_Y), :], low, high, pack)


def half_spec():
    return pl.BlockSpec((1, HALO, LEV, LANES), lambda i: (i, 0, 0, 0))


def pack_spec():
    return pl.BlockSpec((1, ROWS_Y, STRIP, LANES), lambda i: (i, 0, 0, 0))


def half_shape(n):
    return jax.ShapeDtypeStruct((n, HALO, LEV + STRIP, LANES), f32)


def pack_shape(n):
    return jax.ShapeDtypeStruct((n, ROWS_Y, STRIP, LANES), f32)


def prep(canopy, first, n):
    return pl.pallas_call(
        prep_kernel,
        grid=(n,),
        in_specs=[pl.BlockSpec((1, LEV * ROWS_Y, LANES), lambda i: (i + first, 0, 0))],
        out_specs=[half_spec(), half_spec(), pack_spec()],
        out_shape=[half_shape(n), half_shape(n), pack_shape(n)],
        compiler_params=params(),
        name="prep",
    )(canopy)


def scatter_kernel(recv, canopy, counts, low, high, pack, aux_s, xt):
    aux = recv[pl.ds(CAP // 2, DEV, stride=FLUX_ROWS), :]
    aux_s[...] = aux

    def group(g, carry):
        start = pl.multiple_of(g * 16, 16)
        mine = aux_s[pl.ds(start, 16), :]
        lane = lax.broadcasted_iota(jnp.int32, (16, LANES), 1).astype(f32)
        for r in range(CAP):
            cols = [
                jnp.broadcast_to(mine[:, AUX * r + 2 + f : AUX * r + 3 + f], (16, LANES)) - lane
                for f in range(FOOT)
            ]
            for y in range(ROWS_Y):
                n = jnp.zeros((16, LANES), f32)
                for c in cols:
                    n = n + jnp.where(c == float(y * LANES), 1.0, 0.0)
                counts[r, pl.ds(start, 16), y * LANES : (y + 1) * LANES] = n.astype(bf16)
        return carry

    lax.fori_loop(0, DEV // 16, group, 0)
    left = lax.broadcasted_iota(jnp.int32, (DEV, LANES), 1) < LEV
    for p in range(CAP // 2):
        rows = recv[pl.ds(p, DEV, stride=FLUX_ROWS), :]
        turned = pltpu.roll(rows, LEV, 1)
        for odd in range(2):
            r = 2 * p + odd
            area = jnp.where(left, turned, rows) if odd else jnp.where(left, rows, turned)
            factor = jnp.where(
                left,
                jnp.broadcast_to(aux[:, AUX * r : AUX * r + 1], (DEV, LANES)),
                jnp.broadcast_to(aux[:, AUX * r + 1 : AUX * r + 2], (DEV, LANES)),
            )
            hi, lo = halves((area * factor).T)
            xt[:DEV, r * DEV : (r + 1) * DEV] = hi
            xt[DEV:, r * DEV : (r + 1) * DEV] = lo
    table = counts[...].reshape(CAP * DEV, ROWS_Y * LANES)
    both = mm(xt[...], table, NN)
    sums = both[:DEV] + both[DEV:]
    for y in range(ROWS_Y):
        c = canopy[0, pl.ds(y, LEV, stride=ROWS_Y), :]
        p = sums[:LEV, y * LANES : (y + 1) * LANES]
        q = sums[LEV:, y * LANES : (y + 1) * LANES]
        emit_row(y, c + (source_rate / FOOT) * (p - q * c), low, high, pack)


def scatter(recv, canopy):
    return pl.pallas_call(
        scatter_kernel,
        grid=(1,),
        in_specs=[
            whole((DEV * FLUX_ROWS, LANES)),
            pl.BlockSpec((1, LEV * ROWS_Y, LANES), lambda i: (0, 0, 0)),
        ],
        out_specs=[whole((CAP, DEV, ROWS_Y * LANES)), half_spec(), half_spec(), pack_spec()],
        out_shape=[
            jax.ShapeDtypeStruct((CAP, DEV, ROWS_Y * LANES), bf16),
            half_shape(1),
            half_shape(1),
            pack_shape(1),
        ],
        scratch_shapes=[pltpu.VMEM((DEV, LANES), f32), pltpu.VMEM((2 * DEV, CAP * DEV), bf16)],
        compiler_params=params(),
        name="scatter",
    )(recv, canopy)


def merge_kernel(pack, west, east, low_in, high_in, low, high):
    slot = lane_slot() % 16
    for y in range(ROWS_Y):
        strip = jnp.where(
            slot < 4,
            pltpu.roll(west[0, y], LANES - 8, 1),
            jnp.where(slot < 12, pack[0, y], pltpu.roll(east[0, y], 8, 1)),
        )
        dst = low if y < HALO else high
        dst[0, y % HALO] = strip


def merge(pack, west, east, low, high):
    n = pack.shape[0]
    strip_spec = pl.BlockSpec((1, HALO, STRIP, LANES), lambda i: (i, 0, LEV // STRIP, 0))
    anywhere = pl.BlockSpec(memory_space=pl.ANY)
    return pl.pallas_call(
        merge_kernel,
        grid=(n,),
        in_specs=[pack_spec(), pack_spec(), pack_spec(), anywhere, anywhere],
        out_specs=[strip_spec, strip_spec],
        out_shape=[half_shape(n), half_shape(n)],
        input_output_aliases={3: 0, 4: 1},
        compiler_params=params(),
        name="merge",
    )(pack, west, east, low, high)


def exchange(low, high, pack):
    def shifts(axis):
        up = [(i, i + 1) for i in range(lax.axis_size(axis) - 1)]
        return up, [(j, i) for i, j in up]

    up, down = shifts("gx")
    west, east = lax.ppermute(pack, "gx", up), lax.ppermute(pack, "gx", down)
    low, high = merge(pack, west, east, low, high)
    up, down = shifts("gy")
    south, north = lax.ppermute(high, "gy", up), lax.ppermute(low, "gy", down)
    return south, low, high, north


def substeps(parts, coef, coef_strip, edge, buf, strips, put):
    lane = lane_slot()
    sub = lax.broadcasted_iota(jnp.int32, (8, LANES), 0)
    slot = lane % 16
    first, last = lane == 0, lane == LANES - 1
    inside = jnp.where(slot < 4, edge[2], jnp.where(slot < 12, 1.0, edge[3]))
    total = ROWS_Y + 2 * HALO

    def keep(row, value):
        if row < HALO:
            return value * edge[0]
        if row >= HALO + ROWS_Y:
            return value * edge[1]
        return value

    for step in range(1, SUB + 1):
        old, new = (step + 1) % 2, step % 2

        def main(row, start):
            if step == 1:
                return parts[row // HALO][0, row % HALO, start : start + 8, :]
            return buf[old, row, start : start + 8, :]

        def strip(row):
            if step == 1:
                return parts[row // HALO][0, row % HALO, LEV : LEV + STRIP, :]
            return strips[old, row]

        rows = range(step, total - step)
        for i in range(8):
            at = 8 * i
            c0, cw, ce, cs, cn = (coef[k, at : at + 8, :] for k in range(5))
            here, after = main(step - 1, at), main(step, at)
            for row in rows:
                before, here, after = here, after, main(row + 1, at)
                if i == 0:
                    below = jnp.where(sub == 0, here, pltpu.roll(here, 1, 0))
                else:
                    below = main(row, at - 1)
                if i == 7:
                    above = jnp.where(sub == 7, here, pltpu.roll(here, 7, 0))
                else:
                    above = main(row, at + 1)
                side = strip(row)
                left = jnp.where(first, pltpu.roll(side, (LANES - 16 * i - 3) % LANES, 1), pltpu.roll(here, 1, 1))
                right = jnp.where(
                    last,
                    pltpu.roll(side, (LANES - 1 - 16 * i - 12) % LANES, 1),
                    pltpu.roll(here, LANES - 1, 1),
                )
                value = (
                    (c0 * here + cw * left)
                    + (ce * right + cs * before)
                    + (cn * after + vertical_rate * (above + below))
                )
                if step == SUB:
                    put(row - HALO, at, value)
                else:
                    buf[new, row, at : at + 8, :] = keep(row, value)
        if step == SUB:
            break
        c0, cw, ce, cs, cn = (coef_strip[k] for k in range(5))
        here, after = strip(step - 1), strip(step)
        for row in rows:
            before, here, after = here, after, strip(row + 1)
            down = pltpu.roll(here, 1, 0)
            below = jnp.where(sub == 0, jnp.where(lane < 16, here, pltpu.roll(down, 16, 1)), down)
            lift = pltpu.roll(here, 7, 0)
            above = jnp.where(sub == 7, jnp.where(lane >= LANES - 16, here, pltpu.roll(lift, LANES - 16, 1)), lift)
            value = (
                (c0 * here + cw * pltpu.roll(here, 1, 1))
                + (ce * pltpu.roll(here, LANES - 1, 1) + cs * before)
                + (cn * after + vertical_rate * (above + below))
            )
            strips[new, row] = keep(row, value * inside)


def quarter_spec(first):
    return pl.BlockSpec((1, HALO, LEV + STRIP, LANES), lambda i: (i + first, 0, 0, 0))


STENCIL_SCRATCH = [
    (2, ROWS_Y + 2 * HALO, LEV, LANES),
    (2, ROWS_Y + 2 * HALO, STRIP, LANES),
]


def coef_specs():
    return [
        whole((5, LEV, LANES)),
        whole((5, STRIP, LANES)),
        pl.BlockSpec(memory_space=pltpu.SMEM),
    ]


def fields_kernel(*refs):
    south, low, high, north, coef, coef_strip, edge = refs[:7]
    out, buf, strips = refs[-3:]

    def put(y, at, value):
        out[0, pl.ds(at * ROWS_Y + y, 8, stride=ROWS_Y), :] = value

    substeps((south, low, high, north), coef, coef_strip, edge, buf, strips, put)


def fields(parts, coefs, first, n, into=None):
    operands = [*parts, *coefs]
    specs = [quarter_spec(first) for _ in parts] + coef_specs()
    alias = {}
    if into is not None:
        alias = {len(operands): 0}
        operands.append(into)
        specs.append(pl.BlockSpec(memory_space=pl.ANY))
    return pl.pallas_call(
        fields_kernel,
        grid=(n,),
        in_specs=specs,
        out_specs=pl.BlockSpec((1, LEV * ROWS_Y, LANES), lambda i: (i + first + 1, 0, 0)),
        out_shape=jax.ShapeDtypeStruct((8, LEV * ROWS_Y, LANES), f32),
        scratch_shapes=[pltpu.VMEM(s, f32) for s in STENCIL_SCRATCH],
        input_output_aliases=alias,
        compiler_params=params(),
        name="fields",
    )(*operands)


def gather_kernel(south, low, high, north, coef, coef_strip, edge, counts, humid, out, back, buf, strips, table):
    def put(y, at, value):
        out[0, pl.ds(at * ROWS_Y + y, 8, stride=ROWS_Y), :] = value

    substeps((south, low, high, north), coef, coef_strip, edge, buf, strips, put)
    for y in range(ROWS_Y):
        cols = slice(y * LANES, (y + 1) * LANES)
        for k, src in enumerate((out, humid)):
            hi, lo = halves(src[0, pl.ds(y, LEV, stride=ROWS_Y), :] * (1.0 / FOOT))
            table[k * LEV : (k + 1) * LEV, cols] = hi
            table[2 * LEV + k * LEV : 2 * LEV + (k + 1) * LEV, cols] = lo
    for r in range(CAP):
        both = mm(counts[r], table[...], NT)
        back[pl.ds(r, DEV, stride=CAP), :] = both[:, : 2 * LEV] + both[:, 2 * LEV :]


def gather(parts, coefs, counts, into):
    field_block = (1, LEV * ROWS_Y, LANES)
    return pl.pallas_call(
        gather_kernel,
        grid=(1,),
        in_specs=[quarter_spec(0) for _ in parts]
        + coef_specs()
        + [whole((CAP, DEV, ROWS_Y * LANES)), pl.BlockSpec(field_block, lambda i: (1, 0, 0))],
        out_specs=[pl.BlockSpec(field_block, lambda i: (0, 0, 0)), whole((DEV * CAP, LANES))],
        out_shape=[
            jax.ShapeDtypeStruct((8, LEV * ROWS_Y, LANES), f32),
            jax.ShapeDtypeStruct((DEV * CAP, LANES), f32),
        ],
        scratch_shapes=[pltpu.VMEM(s, f32) for s in STENCIL_SCRATCH]
        + [pltpu.VMEM((4 * LEV, ROWS_Y * LANES), bf16)],
        input_output_aliases={8: 0},
        compiler_params=params(),
        name="gather",
    )(*parts, *coefs, counts, into)


def walls_kernel(inverses, walls, package, out, column, a, b_hi, b_lo):
    n = walls.shape[1]

    @pl.when(pl.program_id(0) == 0)
    def _():
        chosen = jnp.zeros((n, NB), f32)
        for p in range(PKG):
            inv = inverses[p]
            hi, lo = halves(inv)
            a[:n, p * n : (p + 1) * n] = hi
            a[n:, p * n : (p + 1) * n] = lo
            chosen = jnp.where(package[...] == p, jnp.broadcast_to(inv[:, 0:1], (n, NB)), chosen)
        column[...] = chosen

    w = walls[0]
    w_hi = w.astype(bf16).astype(f32)
    w_lo = w - w_hi
    for p in range(PKG):
        mine = package[...] == p
        b_hi[p * n : (p + 1) * n, :] = jnp.where(mine, w_hi, 0.0).astype(bf16)
        b_lo[p * n : (p + 1) * n, :] = jnp.where(mine, w_lo, 0.0).astype(bf16)
    both = mm(a[...], b_hi[...], NN)
    out[0] = both[:n] + both[n:] + mm(a[:n, :], b_lo[...], NN)


def walls_product(inverses, walls, package):
    s, n, _ = walls.shape
    return pl.pallas_call(
        walls_kernel,
        grid=(s,),
        in_specs=[
            whole((PKG, n, n)),
            pl.BlockSpec((1, n, NB), lambda i: (i, 0, 0)),
            whole((1, NB)),
        ],
        out_specs=[pl.BlockSpec((1, n, NB), lambda i: (i, 0, 0)), whole((n, NB))],
        out_shape=[jax.ShapeDtypeStruct((s, n, NB), f32), jax.ShapeDtypeStruct((n, NB), f32)],
        scratch_shapes=[
            pltpu.VMEM((2 * n, PKG * n), bf16),
            pltpu.VMEM((PKG * n, NB), bf16),
            pltpu.VMEM((PKG * n, NB), bf16),
        ],
        compiler_params=params(),
        name="walls",
    )(inverses, walls, package)


def final_kernel(recv, code, facade, coeff, walls, product, column, air_out, walls_out, xt):
    picks = []
    for r in range(CAP):
        hi, lo = halves(recv[pl.ds(r, DEV, stride=CAP), :].T)
        xt[:LANES, r * DEV : (r + 1) * DEV] = hi
        xt[LANES:, r * DEV : (r + 1) * DEV] = lo
        picks.append(jnp.where(code[...] == float(r), 1.0, 0.0).astype(bf16))
    both = mm(xt[...], jnp.concatenate(picks, axis=0), NN)
    air = both[:LANES] + both[LANES:]
    air_out[...] = air
    area = facade[...]
    temp = jnp.sum(area * air[:LEV], axis=0, keepdims=True) / jnp.sum(area, axis=0, keepdims=True)
    for s in range(walls_out.shape[0]):
        source = wall_gain * coeff[s : s + 1, :] * (temp - walls[s, 0:1, :])
        walls_out[s] = product[s] + column[...] * source


def final(recv, code, facade, coeff, walls, product, column):
    s, n, _ = walls.shape
    return pl.pallas_call(
        final_kernel,
        grid=(1,),
        in_specs=[
            whole((DEV * CAP, LANES)),
            whole((DEV, NB)),
            whole((LEV, NB)),
            whole((s, NB)),
            pl.BlockSpec((s, 8, NB), lambda _: (0, 0, 0)),
            whole((s, n, NB)),
            whole((n, NB)),
        ],
        out_specs=[whole((2 * LEV, NB)), whole((s, n, NB))],
        out_shape=[
            jax.ShapeDtypeStruct((2 * LEV, NB), f32),
            jax.ShapeDtypeStruct((s, n, NB), f32),
        ],
        scratch_shapes=[pltpu.VMEM((2 * LANES, CAP * DEV), bf16)],
        compiler_params=params(),
        name="final",
    )(recv, code, facade, coeff, walls, product, column)


def transpose_all(x, rows):
    y = lax.all_to_all(
        x.reshape(DEV, 1, rows * LANES), ("gx", "gy"), split_axis=0, concat_axis=0, tiled=True
    )
    return y.reshape(DEV * rows, LANES)


def coefficients(courant):
    cx, cy = courant[0], courant[1]
    c = jnp.stack(
        [
            1.0 - jnp.abs(cx) - jnp.abs(cy) - 4.0 * kappa_rate - 2.0 * vertical_rate,
            jnp.maximum(cx, 0.0) + kappa_rate,
            kappa_rate - jnp.minimum(cx, 0.0),
            jnp.maximum(cy, 0.0) + kappa_rate,
            kappa_rate - jnp.minimum(cy, 0.0),
        ]
    )
    main = jnp.broadcast_to(c[:, :, None], (5, LEV, LANES))
    strip = jnp.broadcast_to(c.reshape(5, 8, 8).transpose(0, 2, 1)[..., None], (5, 8, 8, 16))
    gx, gy = lax.axis_index("gx"), lax.axis_index("gy")
    edge = jnp.stack(
        [gy > 0, gy < lax.axis_size("gy") - 1, gx > 0, gx < lax.axis_size("gx") - 1]
    ).astype(f32)
    return main, strip.reshape(5, STRIP, LANES), edge


def body(canopy, courant, walls, inverses, package, surf_coeff, facade_area, anchor, footprint):
    shape = canopy.shape
    canopy = canopy.reshape(shape[0], LEV * ROWS_Y, LANES)
    send, code = payload(anchor.T, footprint.T, surf_coeff, walls, facade_area)
    recv = transpose_all(send, FLUX_ROWS)
    coefs = coefficients(courant)
    rest = exchange(*prep(canopy, 1, shape[0] - 1))
    out = fields(rest, coefs, 0, EARLY)
    product, column = walls_product(inverses, walls, package[None, :])
    counts, low, high, pack = scatter(recv, canopy)
    zeroth = exchange(low, high, pack)
    out, back = gather(zeroth, coefs, counts, out)
    returned = transpose_all(back, CAP)
    if EARLY < shape[0] - 1:
        out = fields(rest, coefs, EARLY, shape[0] - 1 - EARLY, out)
    air, walls_out = final(returned, code, facade_area, surf_coeff, walls, product, column)
    return out.reshape(shape), air.reshape(2, LEV, NB), walls_out


def solution(mesh):
    placed = (
        P(None, None, "gy", "gx"),
        P(),
        P(None, None, ("gx", "gy")),
        P(),
        P(("gx", "gy")),
        P(None, ("gx", "gy")),
        P(None, ("gx", "gy")),
        P(("gx", "gy"), None),
        P(("gx", "gy"), None),
    )
    return jax.shard_map(
        body,
        mesh=mesh,
        in_specs=placed,
        out_specs=(
            P(None, None, "gy", "gx"),
            P(None, None, ("gx", "gy")),
            P(None, None, ("gx", "gy")),
        ),
        check_vma=False,
    )
```

```python
import functools

import jax
import jax.numpy as jnp
from jax import lax
from jax.experimental import pallas as pl
from jax.experimental.pallas import tpu as pltpu
from jax.sharding import PartitionSpec as P

PKG = 8
SUB = 4
HALO = 4
CAP = 10
FOOT = 8
DEV = 128
LEV = 64
NB = 256
ROWS_Y = 8
LANES = 128
FLUX_ROWS = 6
STRIP = 8
AUX = 2 + FOOT
EARLY = 1

source_rate = 0.1
kappa_rate = 0.05
vertical_rate = 0.05
wall_gain = 0.5

f32 = jnp.float32
bf16 = jnp.bfloat16
VMEM = 16 * 1024 * 1024
NT = (((1,), (1,)), ((), ()))
NN = (((1,), (0,)), ((), ()))


def params(**kw):
    return pltpu.CompilerParams(vmem_limit_bytes=VMEM, **kw)


def whole(shape):
    return pl.BlockSpec(shape, lambda *_: (0,) * len(shape))


def halves(x):
    hi = x.astype(bf16)
    lo = (x - hi.astype(f32)).astype(bf16)
    return hi, lo


def mm(a, b, dims):
    return lax.dot_general(a, b, dims, preferred_element_type=f32)


def payload_kernel(anchor, foot, coeff, walls, facade, out, code_out, aux):
    owner = lax.broadcasted_iota(jnp.int32, (DEV, NB), 0) == anchor[...]
    earlier = lax.broadcasted_iota(jnp.int32, (NB, NB), 0) < lax.broadcasted_iota(
        jnp.int32, (NB, NB), 1
    )
    rank = mm(jnp.where(owner, 1.0, 0.0).astype(bf16), jnp.where(earlier, 1.0, 0.0).astype(bf16), NN)
    code = jnp.where(owner, rank, -1.0)
    code_out[...] = code
    heat = jnp.sum(coeff[...] * walls[:, 0, :], axis=0, keepdims=True)
    coupling = jnp.sum(coeff[...], axis=0, keepdims=True)
    cells = foot[...].astype(f32)
    picks = [jnp.where(code == float(r), 1.0, 0.0).astype(bf16) for r in range(CAP)]
    hi, lo = halves(facade[...])
    zero = jnp.zeros((LEV, NB), bf16)
    even = jnp.concatenate([picks[2 * p] for p in range(CAP // 2)], axis=0)
    odd = jnp.concatenate([picks[2 * p + 1] for p in range(CAP // 2)], axis=0)
    rows = (
        mm(even, jnp.concatenate([hi, zero], axis=0), NT)
        + mm(odd, jnp.concatenate([zero, hi], axis=0), NT)
        + mm(even, jnp.concatenate([lo, zero], axis=0), NT)
        + mm(odd, jnp.concatenate([zero, lo], axis=0), NT)
    )
    for p in range(CAP // 2):
        out[pl.ds(p, DEV, stride=FLUX_ROWS), :] = rows[p * DEV : (p + 1) * DEV]
    aux[...] = jnp.zeros_like(aux)
    for r in range(CAP):
        aux[r, AUX * r : AUX * r + 1, :] = heat
        aux[r, AUX * r + 1 : AUX * r + 2, :] = coupling
        aux[r, AUX * r + 2 : AUX * r + AUX, :] = cells
    total = jnp.zeros((DEV, LANES), f32)
    for r in range(CAP):
        hi, lo = halves(aux[r])
        total = total + mm(picks[r], hi, NT) + mm(picks[r], lo, NT)
    out[pl.ds(CAP // 2, DEV, stride=FLUX_ROWS), :] = total


def payload(anchor, foot, coeff, walls, facade):
    return pl.pallas_call(
        payload_kernel,
        grid=(1,),
        in_specs=[
            whole((1, NB)),
            whole((FOOT, NB)),
            whole((6, NB)),
            pl.BlockSpec((6, 8, NB), lambda _: (0, 0, 0)),
            whole((LEV, NB)),
        ],
        out_specs=[whole((DEV * FLUX_ROWS, LANES)), whole((DEV, NB))],
        out_shape=[
            pltpu.HBM((DEV * FLUX_ROWS, LANES), f32),
            pltpu.HBM((DEV, NB), f32),
        ],
        scratch_shapes=[pltpu.VMEM((CAP, LANES, NB), f32)],
        compiler_params=params(),
        name="payload",
    )(anchor, foot, coeff, walls, facade)


def lane_slot():
    return lax.broadcasted_iota(jnp.int32, (8, LANES), 1)


def pack_row(blocks):
    lane = lane_slot()
    slot = lane % 16
    out = jnp.zeros((8, LANES), f32)
    for i, block in enumerate(blocks):
        here = lane // 16 == i
        west = here & (slot >= 4) & (slot < 8)
        east = here & (slot >= 8) & (slot < 12)
        out = jnp.where(west, pltpu.roll(block, (16 * i + 4) % LANES, 1), out)
        out = jnp.where(east, pltpu.roll(block, (16 * i + 12) % LANES, 1), out)
    return out


def emit_row(y, field, low, high, pack):
    dst = low if y < HALO else high
    dst[0, y % HALO, :, :] = field
    pack[0, y] = pack_row([field[8 * i : 8 * i + 8] for i in range(8)])


def prep_kernel(courant, canopy, low, high, pack, coef, coef_strip):
    for y in range(ROWS_Y):
        emit_row(y, canopy[0, pl.ds(y, LEV, stride=ROWS_Y), :], low, high, pack)

    @pl.when(pl.program_id(0) == 0)
    def _():
        square = (LEV, LEV)
        diagonal = lax.broadcasted_iota(jnp.int32, square, 0) == lax.broadcasted_iota(jnp.int32, square, 1)

        def column(row):
            picked = jnp.where(diagonal, jnp.broadcast_to(courant[row : row + 1, :], square), 0.0)
            return jnp.broadcast_to(jnp.sum(picked, axis=1, keepdims=True), (LEV, LANES))

        cx, cy = column(0), column(1)
        values = (
            1.0 - jnp.abs(cx) - jnp.abs(cy) - (4.0 * kappa_rate + 2.0 * vertical_rate),
            jnp.maximum(cx, 0.0) + kappa_rate,
            kappa_rate - jnp.minimum(cx, 0.0),
            jnp.maximum(cy, 0.0) + kappa_rate,
            kappa_rate - jnp.minimum(cy, 0.0),
        )
        block = lane_slot() // 16
        for k, v in enumerate(values):
            coef[k] = v
            strip = v[0:8]
            for i in range(1, 8):
                strip = jnp.where(block == i, v[8 * i : 8 * i + 8], strip)
            coef_strip[k] = strip


def half_spec():
    return pl.BlockSpec((1, HALO, LEV, LANES), lambda i: (i, 0, 0, 0))


def pack_spec():
    return pl.BlockSpec((1, ROWS_Y, STRIP, LANES), lambda i: (i, 0, 0, 0))


def half_shape(n):
    return jax.ShapeDtypeStruct((n, HALO, LEV + STRIP, LANES), f32)


def pack_shape(n):
    return jax.ShapeDtypeStruct((n, ROWS_Y, STRIP, LANES), f32)


def prep(courant, canopy, first, n):
    return pl.pallas_call(
        prep_kernel,
        grid=(n,),
        in_specs=[
            whole((2, LEV)),
            pl.BlockSpec((1, LEV * ROWS_Y, LANES), lambda i: (i + first, 0, 0)),
        ],
        out_specs=[
            half_spec(),
            half_spec(),
            pack_spec(),
            whole((5, LEV, LANES)),
            whole((5, STRIP, LANES)),
        ],
        out_shape=[
            half_shape(n),
            half_shape(n),
            pack_shape(n),
            jax.ShapeDtypeStruct((5, LEV, LANES), f32),
            jax.ShapeDtypeStruct((5, STRIP, LANES), f32),
        ],
        compiler_params=params(),
        name="prep",
    )(courant, canopy)


def scatter_kernel(recv, canopy, counts_out, low, high, pack, counts, column_s, field_s, xt, field0, sems):
    load = pltpu.make_async_copy(canopy.at[0], field0, sems.at[0])
    load.start()
    aux = recv[pl.ds(CAP // 2, DEV, stride=FLUX_ROWS), :].T
    cell = aux.astype(jnp.int32)
    column_s[...] = cell & (LANES - 1)
    field_s[...] = lax.shift_left(jnp.ones_like(cell), lax.shift_right_logical(cell, jnp.full_like(cell, 5)) & 28)

    def group(g, carry):
        start = pl.multiple_of(g * 16, 16)
        x = lax.broadcasted_iota(jnp.int32, (16, LANES), 0) + start
        for r in range(CAP):
            packed = jnp.zeros((16, LANES), jnp.int32)
            for k in range(AUX * r + 2, AUX * r + AUX):
                here = jnp.broadcast_to(column_s[k : k + 1, :], (16, LANES)) == x
                packed = packed + jnp.where(here, jnp.broadcast_to(field_s[k : k + 1, :], (16, LANES)), 0)
            for y in range(ROWS_Y):
                n = lax.shift_right_logical(packed, jnp.full_like(packed, 4 * y)) & 15
                row = pl.multiple_of(y * LANES + start, 16)
                counts[pl.ds(row, 16), r * DEV : (r + 1) * DEV] = n.astype(f32).astype(bf16)
        return carry

    lax.fori_loop(0, LANES // 16, group, 0)
    save = pltpu.make_async_copy(counts, counts_out, sems.at[1])
    save.start()
    for p in range(CAP // 2):
        rows = recv[pl.ds(p, DEV, stride=FLUX_ROWS), :].T
        for odd in range(2):
            r = 2 * p + odd
            area = rows[LEV * odd : LEV * (odd + 1)]
            for q in range(2):
                hi, lo = halves(area * aux[AUX * r + q : AUX * r + q + 1, :])
                xt[q * LEV : (q + 1) * LEV, r * DEV : (r + 1) * DEV] = hi
                xt[DEV + q * LEV : DEV + (q + 1) * LEV, r * DEV : (r + 1) * DEV] = lo
    both = mm(xt[...], counts[...], NT)
    sums = both[:DEV] + both[DEV:]
    load.wait()
    for y in range(ROWS_Y):
        c = field0[pl.ds(y, LEV, stride=ROWS_Y), :]
        p = sums[:LEV, y * LANES : (y + 1) * LANES]
        q = sums[LEV:, y * LANES : (y + 1) * LANES]
        emit_row(y, c + (source_rate / FOOT) * (p - q * c), low, high, pack)
    save.wait()


def scatter(recv, canopy):
    return pl.pallas_call(
        scatter_kernel,
        grid=(1,),
        in_specs=[whole((DEV * FLUX_ROWS, LANES)), pl.BlockSpec(memory_space=pltpu.HBM)],
        out_specs=[pl.BlockSpec(memory_space=pltpu.HBM), half_spec(), half_spec(), pack_spec()],
        out_shape=[
            pltpu.HBM((ROWS_Y * LANES, CAP * DEV), bf16),
            half_shape(1),
            half_shape(1),
            pack_shape(1),
        ],
        scratch_shapes=[
            pltpu.VMEM((ROWS_Y * LANES, CAP * DEV), bf16),
            pltpu.VMEM((LANES, DEV), jnp.int32),
            pltpu.VMEM((LANES, DEV), jnp.int32),
            pltpu.VMEM((2 * DEV, CAP * DEV), bf16),
            pltpu.VMEM((LEV * ROWS_Y, LANES), f32),
            pltpu.SemaphoreType.DMA((2,)),
        ],
        compiler_params=params(),
        name="scatter",
    )(recv, canopy)


def merge_kernel(pack, west, east, low_in, high_in, low, high):
    slot = lane_slot() % 16
    for y in range(ROWS_Y):
        strip = jnp.where(
            slot < 4,
            pltpu.roll(west[0, y], LANES - 8, 1),
            jnp.where(slot < 12, pack[0, y], pltpu.roll(east[0, y], 8, 1)),
        )
        dst = low if y < HALO else high
        dst[0, y % HALO] = strip


def merge(pack, west, east, low, high):
    n = pack.shape[0]
    strip_spec = pl.BlockSpec((1, HALO, STRIP, LANES), lambda i: (i, 0, LEV // STRIP, 0))
    anywhere = pl.BlockSpec(memory_space=pl.ANY)
    return pl.pallas_call(
        merge_kernel,
        grid=(n,),
        in_specs=[pack_spec(), pack_spec(), pack_spec(), anywhere, anywhere],
        out_specs=[strip_spec, strip_spec],
        out_shape=[half_shape(n), half_shape(n)],
        input_output_aliases={3: 0, 4: 1},
        compiler_params=params(),
        name="merge",
    )(pack, west, east, low, high)


def shifts(axis):
    up = [(i, i + 1) for i in range(lax.axis_size(axis) - 1)]
    return up, [(j, i) for i, j in up]


def across_x(low, high, pack):
    up, down = shifts("gx")
    west, east = lax.ppermute(pack, "gx", up), lax.ppermute(pack, "gx", down)
    return merge(pack, west, east, low, high)


def across_y(low, high):
    up, down = shifts("gy")
    south, north = lax.ppermute(high, "gy", up), lax.ppermute(low, "gy", down)
    return south, low, high, north


def substeps(parts, coef, coef_strip, edge, buf, strips, ends, put):
    lane = lane_slot()
    sub = lax.broadcasted_iota(jnp.int32, (8, LANES), 0)
    slot = lane % 16
    first, last = lane == 0, lane == LANES - 1
    inside = jnp.where(slot < 4, edge[2], jnp.where(slot < 12, 1.0, edge[3]))
    total = ROWS_Y + 2 * HALO

    def keep(row, value):
        if row < HALO:
            return value * edge[0]
        if row >= HALO + ROWS_Y:
            return value * edge[1]
        return value

    for step in range(1, SUB + 1):
        old, new = (step + 1) % 2, step % 2

        def main(row, start):
            if step == 1:
                return parts[row // HALO][0, row % HALO, start : start + 8, :]
            return buf[old, row, start : start + 8, :]

        def strip(row):
            if step == 1:
                return parts[row // HALO][0, row % HALO, LEV : LEV + STRIP, :]
            return strips[old, row]

        rows = range(step, total - step)
        for row in rows:
            side = strip(row)
            ends[row] = jnp.where(slot == 3, side, pltpu.roll(side, LANES - 10, 1))
        for i in range(8):
            at = 8 * i
            c0, cw, ce, cs, cn = (coef[k, at : at + 8, :] for k in range(5))
            here, after = main(step - 1, at), main(step, at)
            for row in rows:
                before, here, after = here, after, main(row + 1, at)
                if i == 0:
                    below = jnp.where(sub == 0, here, pltpu.roll(here, 1, 0))
                else:
                    below = pltpu.roll(jnp.where(sub == 7, main(row, at - 8), here), 1, 0)
                if i == 7:
                    above = jnp.where(sub == 7, here, pltpu.roll(here, 7, 0))
                else:
                    above = pltpu.roll(jnp.where(sub == 0, main(row, at + 8), here), 7, 0)
                side = pltpu.roll(ends[row], (LANES - 16 * i - 3) % LANES, 1)
                left = jnp.where(first, side, pltpu.roll(here, 1, 1))
                right = jnp.where(last, side, pltpu.roll(here, LANES - 1, 1))
                value = (
                    (c0 * here + cw * left)
                    + (ce * right + cs * before)
                    + (cn * after + vertical_rate * (above + below))
                )
                if step == SUB:
                    put(row - HALO, at, value)
                else:
                    buf[new, row, at : at + 8, :] = keep(row, value)
        if step == SUB:
            break
        c0, cw, ce, cs, cn = (coef_strip[k] for k in range(5))
        here, after = strip(step - 1), strip(step)
        for row in rows:
            before, here, after = here, after, strip(row + 1)
            down = pltpu.roll(here, 1, 0)
            below = jnp.where(sub == 0, jnp.where(lane < 16, here, pltpu.roll(down, 16, 1)), down)
            lift = pltpu.roll(here, 7, 0)
            above = jnp.where(sub == 7, jnp.where(lane >= LANES - 16, here, pltpu.roll(lift, LANES - 16, 1)), lift)
            value = (
                (c0 * here + cw * pltpu.roll(here, 1, 1))
                + (ce * pltpu.roll(here, LANES - 1, 1) + cs * before)
                + (cn * after + vertical_rate * (above + below))
            )
            strips[new, row] = keep(row, value * inside)


def quarter_spec(first):
    return pl.BlockSpec((1, HALO, LEV + STRIP, LANES), lambda i: (i + first, 0, 0, 0))


STENCIL_SCRATCH = [
    (2, ROWS_Y + 2 * HALO, LEV, LANES),
    (2, ROWS_Y + 2 * HALO, STRIP, LANES),
    (ROWS_Y + 2 * HALO, STRIP, LANES),
]


def coef_specs():
    return [
        whole((5, LEV, LANES)),
        whole((5, STRIP, LANES)),
        pl.BlockSpec(memory_space=pltpu.SMEM),
    ]


def fields_kernel(*refs):
    south, low, high, north, coef, coef_strip, edge = refs[:7]
    out, buf, strips, ends = refs[-4:]

    def put(y, at, value):
        out[0, pl.ds(at * ROWS_Y + y, 8, stride=ROWS_Y), :] = value

    substeps((south, low, high, north), coef, coef_strip, edge, buf, strips, ends, put)


def fields(parts, coefs, first, n, into=None):
    operands = [*parts, *coefs]
    specs = [quarter_spec(first) for _ in parts] + coef_specs()
    alias = {}
    if into is not None:
        alias = {len(operands): 0}
        operands.append(into)
        specs.append(pl.BlockSpec(memory_space=pl.ANY))
    return pl.pallas_call(
        fields_kernel,
        grid=(n,),
        in_specs=specs,
        out_specs=pl.BlockSpec((1, LEV * ROWS_Y, LANES), lambda i: (i + first + 1, 0, 0)),
        out_shape=pltpu.HBM((8, LEV * ROWS_Y, LANES), f32),
        scratch_shapes=[pltpu.VMEM(s, f32) for s in STENCIL_SCRATCH],
        input_output_aliases=alias,
        compiler_params=params(),
        name="fields",
    )(*operands)


def gather_kernel(
    south, low, high, north, coef, coef_strip, edge, counts_in, fields_in, out, back, *scratch
):
    buf, strips, ends, table, counts, humid, sems = scratch
    fetch = pltpu.make_async_copy(counts_in, counts, sems.at[0])
    fetch.start()
    other = pltpu.make_async_copy(fields_in.at[1], humid, sems.at[1])
    other.start()

    def put(y, at, value):
        out[0, pl.ds(at * ROWS_Y + y, 8, stride=ROWS_Y), :] = value

    substeps((south, low, high, north), coef, coef_strip, edge, buf, strips, ends, put)
    other.wait()
    for y in range(ROWS_Y):
        cols = slice(y * LANES, (y + 1) * LANES)
        pick = pl.ds(y, LEV, stride=ROWS_Y)
        for k, field in enumerate((out[0, pick, :], humid[pick, :])):
            hi, lo = halves(field * (1.0 / FOOT))
            table[k * LEV : (k + 1) * LEV, cols] = hi
            table[2 * LEV + k * LEV : 2 * LEV + (k + 1) * LEV, cols] = lo
    fetch.wait()
    both = mm(table[...], counts[...], NN)
    sums = both[: 2 * LEV] + both[2 * LEV :]
    for r in range(CAP):
        back[pl.ds(r, DEV, stride=CAP), :] = sums[:, r * DEV : (r + 1) * DEV].T


def gather(parts, coefs, counts, into):
    field_block = (1, LEV * ROWS_Y, LANES)
    remote = pl.BlockSpec(memory_space=pltpu.HBM)
    return pl.pallas_call(
        gather_kernel,
        grid=(1,),
        in_specs=[quarter_spec(0) for _ in parts] + coef_specs() + [remote, remote],
        out_specs=[pl.BlockSpec(field_block, lambda i: (0, 0, 0)), whole((DEV * CAP, LANES))],
        out_shape=[
            pltpu.HBM((8, LEV * ROWS_Y, LANES), f32),
            pltpu.HBM((DEV * CAP, LANES), f32),
        ],
        scratch_shapes=[pltpu.VMEM(s, f32) for s in STENCIL_SCRATCH]
        + [
            pltpu.VMEM((4 * LEV, ROWS_Y * LANES), bf16),
            pltpu.VMEM((ROWS_Y * LANES, CAP * DEV), bf16),
            pltpu.VMEM((LEV * ROWS_Y, LANES), f32),
            pltpu.SemaphoreType.DMA((2,)),
        ],
        input_output_aliases={8: 0},
        compiler_params=params(),
        name="gather",
    )(*parts, *coefs, counts, into)


def walls_kernel(inverses, walls, package, out, column, a, b_hi, b_lo):
    n = walls.shape[1]

    @pl.when(pl.program_id(0) == 0)
    def _():
        chosen = jnp.zeros((n, NB), f32)
        for p in range(PKG):
            inv = inverses[p]
            hi, lo = halves(inv)
            a[:n, p * n : (p + 1) * n] = hi
            a[n:, p * n : (p + 1) * n] = lo
            chosen = jnp.where(package[...] == p, jnp.broadcast_to(inv[:, 0:1], (n, NB)), chosen)
        column[...] = chosen

    w = walls[0]
    w_hi = w.astype(bf16).astype(f32)
    w_lo = w - w_hi
    for p in range(PKG):
        mine = package[...] == p
        b_hi[p * n : (p + 1) * n, :] = jnp.where(mine, w_hi, 0.0).astype(bf16)
        b_lo[p * n : (p + 1) * n, :] = jnp.where(mine, w_lo, 0.0).astype(bf16)
    both = mm(a[...], b_hi[...], NN)
    out[0] = both[:n] + both[n:] + mm(a[:n, :], b_lo[...], NN)


def walls_product(inverses, walls, package):
    s, n, _ = walls.shape
    return pl.pallas_call(
        walls_kernel,
        grid=(s,),
        in_specs=[
            whole((PKG, n, n)),
            pl.BlockSpec((1, n, NB), lambda i: (i, 0, 0)),
            whole((1, NB)),
        ],
        out_specs=[pl.BlockSpec((1, n, NB), lambda i: (i, 0, 0)), whole((n, NB))],
        out_shape=[pltpu.HBM((s, n, NB), f32), pltpu.HBM((n, NB), f32)],
        scratch_shapes=[
            pltpu.VMEM((2 * n, PKG * n), bf16),
            pltpu.VMEM((PKG * n, NB), bf16),
            pltpu.VMEM((PKG * n, NB), bf16),
        ],
        compiler_params=params(),
        name="walls",
    )(inverses, walls, package)


def final_kernel(recv, code, facade, coeff, walls, product, column, air_out, walls_out, xt, value, col, first, sems):
    surfaces = value.shape[0]
    loads = [
        pltpu.make_async_copy(product, value, sems.at[0]),
        pltpu.make_async_copy(column, col, sems.at[1]),
        pltpu.make_async_copy(walls.at[:, pl.ds(0, 8), :], first, sems.at[2]),
    ]
    for c in loads:
        c.start()
    picks = []
    for r in range(CAP):
        hi, lo = halves(recv[pl.ds(r, DEV, stride=CAP), :].T)
        xt[:LANES, r * DEV : (r + 1) * DEV] = hi
        xt[LANES:, r * DEV : (r + 1) * DEV] = lo
        picks.append(jnp.where(code[...] == float(r), 1.0, 0.0).astype(bf16))
    both = mm(xt[...], jnp.concatenate(picks, axis=0), NN)
    air = both[:LANES] + both[LANES:]
    air_out[...] = air
    area = facade[...]
    temp = jnp.sum(area * air[:LEV], axis=0, keepdims=True) / jnp.sum(area, axis=0, keepdims=True)
    for c in loads:
        c.wait()
    saves = []
    for s in range(surfaces):
        source = wall_gain * coeff[s : s + 1, :] * (temp - first[s, 0:1, :])
        value[s] = value[s] + col[...] * source
        saves.append(pltpu.make_async_copy(value.at[s], walls_out.at[s], sems.at[3 + s]))
        saves[s].start()
    for c in saves:
        c.wait()


def final(recv, code, facade, coeff, walls, product, column):
    s, n, _ = walls.shape
    remote = pl.BlockSpec(memory_space=pltpu.HBM)
    return pl.pallas_call(
        final_kernel,
        grid=(1,),
        in_specs=[
            whole((DEV * CAP, LANES)),
            whole((DEV, NB)),
            whole((LEV, NB)),
            whole((s, NB)),
            remote,
            remote,
            remote,
        ],
        out_specs=[whole((2 * LEV, NB)), remote],
        out_shape=[
            jax.ShapeDtypeStruct((2 * LEV, NB), f32),
            pltpu.HBM((s, n, NB), f32),
        ],
        scratch_shapes=[
            pltpu.VMEM((2 * LANES, CAP * DEV), bf16),
            pltpu.VMEM((s, n, NB), f32),
            pltpu.VMEM((n, NB), f32),
            pltpu.VMEM((s, 8, NB), f32),
            pltpu.SemaphoreType.DMA((3 + s,)),
        ],
        compiler_params=params(),
        name="final",
    )(recv, code, facade, coeff, walls, product, column)


def transpose_all(x, rows):
    y = lax.all_to_all(
        x.reshape(DEV, 1, rows * LANES), ("gx", "gy"), split_axis=0, concat_axis=0, tiled=True
    )
    return y.reshape(DEV * rows, LANES)


def inside_edges():
    gx, gy = lax.axis_index("gx"), lax.axis_index("gy")
    side = jnp.arange(4, dtype=jnp.int32)
    place = jnp.where(side < 2, gy, gx)
    limit = jnp.where(side < 2, lax.axis_size("gy") - 1, lax.axis_size("gx") - 1)
    return jnp.where(side % 2 == 0, place > 0, place < limit).astype(f32)


def hbm(x):
    return pltpu.with_memory_space_constraint(x, pltpu.HBM)


def body(canopy, courant, walls, inverses, package, surf_coeff, facade_area, anchor, footprint):
    shape = canopy.shape
    canopy = canopy.reshape(shape[0], LEV * ROWS_Y, LANES)
    edge = inside_edges()
    send, code = payload(anchor.T, footprint.T, surf_coeff, hbm(walls), facade_area)
    recv = transpose_all(send, FLUX_ROWS)
    later, code = lax.optimization_barrier((canopy, code))
    low, high, pack, coef, coef_strip = prep(courant, later, 1, shape[0] - 1)
    coefs = (coef, coef_strip, edge)
    low, high = across_x(low, high, pack)
    recv, low, high = lax.optimization_barrier((recv, low, high))
    rest = across_y(low, high)
    out = fields(rest, coefs, 0, EARLY)
    product, column = walls_product(inverses, walls, package[None, :])
    counts, low, high, pack = scatter(recv, hbm(canopy))
    zeroth = across_y(*across_x(low, high, pack))
    out, back = gather(zeroth, coefs, counts, out)
    returned = transpose_all(back, CAP)
    if EARLY < shape[0] - 1:
        out = fields(rest, coefs, EARLY, shape[0] - 1 - EARLY, out)
    air, walls_out = final(returned, code, facade_area, surf_coeff, hbm(walls), product, column)
    return out.reshape(shape), air.reshape(2, LEV, NB), walls_out


def solution(mesh):
    placed = (
        P(None, None, "gy", "gx"),
        P(),
        P(None, None, ("gx", "gy")),
        P(),
        P(("gx", "gy")),
        P(None, ("gx", "gy")),
        P(None, ("gx", "gy")),
        P(("gx", "gy"), None),
        P(("gx", "gy"), None),
    )
    return jax.shard_map(
        body,
        mesh=mesh,
        in_specs=placed,
        out_specs=(
            P(None, None, "gy", "gx"),
            P(None, None, ("gx", "gy")),
            P(None, None, ("gx", "gy")),
        ),
        check_vma=False,
    )
```

```python
import functools

import jax
import jax.numpy as jnp
from jax import lax
from jax.experimental import pallas as pl
from jax.experimental.pallas import tpu as pltpu
from jax.sharding import PartitionSpec as P

PKG = 8
SUB = 4
HALO = 4
CAP = 10
FOOT = 8
DEV = 128
LEV = 64
NB = 256
ROWS_Y = 8
LANES = 128
FLUX_ROWS = 6
STRIP = 8
AUX = 2 + FOOT
NEAR = 2

source_rate = 0.1
kappa_rate = 0.05
vertical_rate = 0.05
wall_gain = 0.5

f32 = jnp.float32
bf16 = jnp.bfloat16
VMEM = 16 * 1024 * 1024
NT = (((1,), (1,)), ((), ()))
NN = (((1,), (0,)), ((), ()))


def params(**kw):
    return pltpu.CompilerParams(vmem_limit_bytes=VMEM, **kw)


def whole(shape):
    return pl.BlockSpec(shape, lambda *_: (0,) * len(shape))


REMOTE = pl.BlockSpec(memory_space=pltpu.HBM)


def halves(x):
    hi = x.astype(bf16)
    lo = (x - hi.astype(f32)).astype(bf16)
    return hi, lo


def mm(a, b, dims):
    return lax.dot_general(a, b, dims, preferred_element_type=f32)


def payload_kernel(anchor, foot, coeff, walls, facade, out, code_out, aux):
    owner = lax.broadcasted_iota(jnp.int32, (DEV, NB), 0) == anchor[...]
    earlier = lax.broadcasted_iota(jnp.int32, (NB, NB), 0) < lax.broadcasted_iota(
        jnp.int32, (NB, NB), 1
    )
    rank = mm(jnp.where(owner, 1.0, 0.0).astype(bf16), jnp.where(earlier, 1.0, 0.0).astype(bf16), NN)
    code = jnp.where(owner, rank, -1.0)
    code_out[...] = code
    heat = jnp.sum(coeff[...] * walls[:, 0, :], axis=0, keepdims=True)
    coupling = jnp.sum(coeff[...], axis=0, keepdims=True)
    cells = foot[...].astype(f32)
    picks = [jnp.where(code == float(r), 1.0, 0.0).astype(bf16) for r in range(CAP)]
    hi, lo = halves(facade[...])
    zero = jnp.zeros((LEV, NB), bf16)
    even = jnp.concatenate([picks[2 * p] for p in range(CAP // 2)], axis=0)
    odd = jnp.concatenate([picks[2 * p + 1] for p in range(CAP // 2)], axis=0)
    rows = (
        mm(even, jnp.concatenate([hi, zero], axis=0), NT)
        + mm(odd, jnp.concatenate([zero, hi], axis=0), NT)
        + mm(even, jnp.concatenate([lo, zero], axis=0), NT)
        + mm(odd, jnp.concatenate([zero, lo], axis=0), NT)
    )
    for p in range(CAP // 2):
        out[pl.ds(p, DEV, stride=FLUX_ROWS), :] = rows[p * DEV : (p + 1) * DEV]
    aux[...] = jnp.zeros_like(aux)
    for r in range(CAP):
        aux[r, AUX * r : AUX * r + 1, :] = heat
        aux[r, AUX * r + 1 : AUX * r + 2, :] = coupling
        aux[r, AUX * r + 2 : AUX * r + AUX, :] = cells
    total = jnp.zeros((DEV, LANES), f32)
    for r in range(CAP):
        hi, lo = halves(aux[r])
        total = total + mm(picks[r], hi, NT) + mm(picks[r], lo, NT)
    out[pl.ds(CAP // 2, DEV, stride=FLUX_ROWS), :] = total


def payload(anchor, foot, coeff, walls, facade):
    return pl.pallas_call(
        payload_kernel,
        grid=(1,),
        in_specs=[
            whole((1, NB)),
            whole((FOOT, NB)),
            whole((6, NB)),
            pl.BlockSpec((6, 8, NB), lambda _: (0, 0, 0)),
            whole((LEV, NB)),
        ],
        out_specs=[whole((DEV * FLUX_ROWS, LANES)), whole((DEV, NB))],
        out_shape=[
            pltpu.HBM((DEV * FLUX_ROWS, LANES), f32),
            pltpu.HBM((DEV, NB), f32),
        ],
        scratch_shapes=[pltpu.VMEM((CAP, LANES, NB), f32)],
        compiler_params=params(),
        name="payload",
    )(anchor, foot, coeff, walls, facade)


def lane_slot():
    return lax.broadcasted_iota(jnp.int32, (8, LANES), 1)


def pack_row(blocks):
    lane = lane_slot()
    slot = lane % 16
    out = jnp.zeros((8, LANES), f32)
    for i, block in enumerate(blocks):
        here = lane // 16 == i
        west = here & (slot >= 4) & (slot < 8)
        east = here & (slot >= 8) & (slot < 12)
        out = jnp.where(west, pltpu.roll(block, (16 * i + 4) % LANES, 1), out)
        out = jnp.where(east, pltpu.roll(block, (16 * i + 12) % LANES, 1), out)
    return out


def emit_row(f, y, field, low, high, pack):
    dst = low if y < HALO else high
    dst[f, y % HALO, :LEV, :] = field
    pack[f, y] = pack_row([field[8 * i : 8 * i + 8] for i in range(8)])


def prep_kernel(courant_in, canopy, low, high, pack, coef, coef_strip, field, courant, sems):
    n = field.shape[0]
    loads = [pltpu.make_async_copy(canopy.at[NEAR + f], field.at[f], sems.at[f]) for f in range(n)]
    given = pltpu.make_async_copy(courant_in, courant, sems.at[n])
    given.start()
    for c in loads:
        c.start()
    given.wait()
    square = (LEV, LEV)
    diagonal = lax.broadcasted_iota(jnp.int32, square, 0) == lax.broadcasted_iota(jnp.int32, square, 1)

    def column(row):
        picked = jnp.where(diagonal, jnp.broadcast_to(courant[row : row + 1, :], square), 0.0)
        return jnp.broadcast_to(jnp.sum(picked, axis=1, keepdims=True), (LEV, LANES))

    cx, cy = column(0), column(1)
    values = (
        1.0 - jnp.abs(cx) - jnp.abs(cy) - (4.0 * kappa_rate + 2.0 * vertical_rate),
        jnp.maximum(cx, 0.0) + kappa_rate,
        kappa_rate - jnp.minimum(cx, 0.0),
        jnp.maximum(cy, 0.0) + kappa_rate,
        kappa_rate - jnp.minimum(cy, 0.0),
    )
    block = lane_slot() // 16
    for k, v in enumerate(values):
        coef[k] = v
        strip = v[0:8]
        for i in range(1, 8):
            strip = jnp.where(block == i, v[8 * i : 8 * i + 8], strip)
        coef_strip[k] = strip
    for f in range(n):
        loads[f].wait()
        for y in range(ROWS_Y):
            emit_row(f, y, field[f, pl.ds(y, LEV, stride=ROWS_Y), :], low, high, pack)


def half_shape(n):
    return jax.ShapeDtypeStruct((n, HALO, LEV + STRIP, LANES), f32)


def pack_shape(n):
    return jax.ShapeDtypeStruct((n, ROWS_Y, STRIP, LANES), f32)


def half_spec(n):
    return pl.BlockSpec((n, HALO, LEV, LANES), lambda i: (0, 0, 0, 0))


def prep(courant, canopy):
    n = canopy.shape[0] - NEAR
    return pl.pallas_call(
        prep_kernel,
        grid=(1,),
        in_specs=[REMOTE, REMOTE],
        out_specs=[
            half_spec(n),
            half_spec(n),
            whole((n, ROWS_Y, STRIP, LANES)),
            whole((5, LEV, LANES)),
            whole((5, STRIP, LANES)),
        ],
        out_shape=[
            half_shape(n),
            half_shape(n),
            pack_shape(n),
            pltpu.HBM((5, LEV, LANES), f32),
            pltpu.HBM((5, STRIP, LANES), f32),
        ],
        scratch_shapes=[
            pltpu.VMEM((n, LEV * ROWS_Y, LANES), f32),
            pltpu.VMEM((2, LEV), f32),
            pltpu.SemaphoreType.DMA((n + 1,)),
        ],
        compiler_params=params(),
        name="prep",
    )(courant, canopy)


def scatter_kernel(recv, canopy, counts_out, low, high, pack, counts, column_s, field_s, xt, near, sems):
    load = pltpu.make_async_copy(canopy.at[pl.ds(0, NEAR)], near, sems.at[0])
    load.start()
    aux = recv[pl.ds(CAP // 2, DEV, stride=FLUX_ROWS), :].T
    cell = aux.astype(jnp.int32)
    column_s[...] = cell & (LANES - 1)
    field_s[...] = lax.shift_left(jnp.ones_like(cell), lax.shift_right_logical(cell, jnp.full_like(cell, 5)) & 28)

    def group(g, carry):
        start = pl.multiple_of(g * 16, 16)
        x = lax.broadcasted_iota(jnp.int32, (16, LANES), 0) + start
        for r in range(CAP):
            packed = jnp.zeros((16, LANES), jnp.int32)
            for k in range(AUX * r + 2, AUX * r + AUX):
                here = jnp.broadcast_to(column_s[k : k + 1, :], (16, LANES)) == x
                packed = packed + jnp.where(here, jnp.broadcast_to(field_s[k : k + 1, :], (16, LANES)), 0)
            for y in range(ROWS_Y):
                n = lax.shift_right_logical(packed, jnp.full_like(packed, 4 * y)) & 15
                row = pl.multiple_of(y * LANES + start, 16)
                counts[pl.ds(row, 16), r * DEV : (r + 1) * DEV] = n.astype(f32).astype(bf16)
        return carry

    lax.fori_loop(0, LANES // 16, group, 0)
    save = pltpu.make_async_copy(counts, counts_out, sems.at[1])
    save.start()
    for p in range(CAP // 2):
        rows = recv[pl.ds(p, DEV, stride=FLUX_ROWS), :].T
        for odd in range(2):
            r = 2 * p + odd
            area = rows[LEV * odd : LEV * (odd + 1)]
            for q in range(2):
                hi, lo = halves(area * aux[AUX * r + q : AUX * r + q + 1, :])
                xt[q * LEV : (q + 1) * LEV, r * DEV : (r + 1) * DEV] = hi
                xt[DEV + q * LEV : DEV + (q + 1) * LEV, r * DEV : (r + 1) * DEV] = lo
    both = mm(xt[...], counts[...], NT)
    sums = both[:DEV] + both[DEV:]
    load.wait()
    for y in range(ROWS_Y):
        c = near[0, pl.ds(y, LEV, stride=ROWS_Y), :]
        p = sums[:LEV, y * LANES : (y + 1) * LANES]
        q = sums[LEV:, y * LANES : (y + 1) * LANES]
        emit_row(0, y, c + (source_rate / FOOT) * (p - q * c), low, high, pack)
        for f in range(1, NEAR):
            emit_row(f, y, near[f, pl.ds(y, LEV, stride=ROWS_Y), :], low, high, pack)
    save.wait()


def scatter(recv, canopy):
    return pl.pallas_call(
        scatter_kernel,
        grid=(1,),
        in_specs=[whole((DEV * FLUX_ROWS, LANES)), pl.BlockSpec(memory_space=pltpu.HBM)],
        out_specs=[
            REMOTE,
            half_spec(NEAR),
            half_spec(NEAR),
            whole((NEAR, ROWS_Y, STRIP, LANES)),
        ],
        out_shape=[
            pltpu.HBM((ROWS_Y * LANES, CAP * DEV), bf16),
            half_shape(NEAR),
            half_shape(NEAR),
            pack_shape(NEAR),
        ],
        scratch_shapes=[
            pltpu.VMEM((ROWS_Y * LANES, CAP * DEV), bf16),
            pltpu.VMEM((LANES, DEV), jnp.int32),
            pltpu.VMEM((LANES, DEV), jnp.int32),
            pltpu.VMEM((2 * DEV, CAP * DEV), bf16),
            pltpu.VMEM((NEAR, LEV * ROWS_Y, LANES), f32),
            pltpu.SemaphoreType.DMA((2,)),
        ],
        compiler_params=params(),
        name="scatter",
    )(recv, canopy)


def merge_kernel(pack, west, east, low_in, high_in, low, high):
    slot = lane_slot() % 16
    for f in range(pack.shape[0]):
        for y in range(ROWS_Y):
            strip = jnp.where(
                slot < 4,
                pltpu.roll(west[f, y], LANES - 8, 1),
                jnp.where(slot < 12, pack[f, y], pltpu.roll(east[f, y], 8, 1)),
            )
            dst = low if y < HALO else high
            dst[f, y % HALO] = strip


def merge(pack, west, east, low, high):
    n = pack.shape[0]
    pack_spec = whole((n, ROWS_Y, STRIP, LANES))
    strip_spec = pl.BlockSpec((n, HALO, STRIP, LANES), lambda i: (0, 0, LEV // STRIP, 0))
    anywhere = pl.BlockSpec(memory_space=pl.ANY)
    return pl.pallas_call(
        merge_kernel,
        grid=(1,),
        in_specs=[pack_spec, pack_spec, pack_spec, anywhere, anywhere],
        out_specs=[strip_spec, strip_spec],
        out_shape=[half_shape(n), half_shape(n)],
        input_output_aliases={3: 0, 4: 1},
        compiler_params=params(),
        name="merge",
    )(pack, west, east, low, high)


def shifts(axis):
    up = [(i, i + 1) for i in range(lax.axis_size(axis) - 1)]
    return up, [(j, i) for i, j in up]


def across_x(low, high, pack, beside=None):
    up, down = shifts("gx")
    west, east = lax.ppermute(pack, "gx", up), lax.ppermute(pack, "gx", down)
    done = None
    if beside is not None:
        done = beside()
        west, east, done = lax.optimization_barrier((west, east, done))
    low, high = merge(pack, west, east, low, high)
    return low, high, done


def across_y(low, high):
    up, down = shifts("gy")
    south, north = lax.ppermute(high, "gy", up), lax.ppermute(low, "gy", down)
    return south, low, high, north


def substeps(f, parts, coef, coef_strip, edge, buf, strips, ends, put):
    lane = lane_slot()
    sub = lax.broadcasted_iota(jnp.int32, (8, LANES), 0)
    slot = lane % 16
    first, last = lane == 0, lane == LANES - 1
    inside = jnp.where(slot < 4, edge[2], jnp.where(slot < 12, 1.0, edge[3]))
    total = ROWS_Y + 2 * HALO

    def keep(row, value):
        if row < HALO:
            return value * edge[0]
        if row >= HALO + ROWS_Y:
            return value * edge[1]
        return value

    for step in range(1, SUB + 1):
        old, new = (step + 1) % 2, step % 2

        def main(row, start):
            if step == 1:
                return parts[row // HALO][f, row % HALO, start : start + 8, :]
            return buf[old, row, start : start + 8, :]

        def strip(row):
            if step == 1:
                return parts[row // HALO][f, row % HALO, LEV : LEV + STRIP, :]
            return strips[old, row]

        rows = range(step, total - step)
        for row in rows:
            side = strip(row)
            ends[row] = jnp.where(slot == 3, side, pltpu.roll(side, LANES - 10, 1))
        for i in range(8):
            at = 8 * i
            c0, cw, ce, cs, cn = (coef[k, at : at + 8, :] for k in range(5))
            here, after = main(step - 1, at), main(step, at)
            for row in rows:
                before, here, after = here, after, main(row + 1, at)
                if i == 0:
                    below = jnp.where(sub == 0, here, pltpu.roll(here, 1, 0))
                else:
                    below = pltpu.roll(jnp.where(sub == 7, main(row, at - 8), here), 1, 0)
                if i == 7:
                    above = jnp.where(sub == 7, here, pltpu.roll(here, 7, 0))
                else:
                    above = pltpu.roll(jnp.where(sub == 0, main(row, at + 8), here), 7, 0)
                side = pltpu.roll(ends[row], (LANES - 16 * i - 3) % LANES, 1)
                left = jnp.where(first, side, pltpu.roll(here, 1, 1))
                right = jnp.where(last, side, pltpu.roll(here, LANES - 1, 1))
                value = (
                    (c0 * here + cw * left)
                    + (ce * right + cs * before)
                    + (cn * after + vertical_rate * (above + below))
                )
                if step == SUB:
                    put(row - HALO, at, value)
                else:
                    buf[new, row, at : at + 8, :] = keep(row, value)
        if step == SUB:
            break
        c0, cw, ce, cs, cn = (coef_strip[k] for k in range(5))
        here, after = strip(step - 1), strip(step)
        for row in rows:
            before, here, after = here, after, strip(row + 1)
            down = pltpu.roll(here, 1, 0)
            below = jnp.where(sub == 0, jnp.where(lane < 16, here, pltpu.roll(down, 16, 1)), down)
            lift = pltpu.roll(here, 7, 0)
            above = jnp.where(sub == 7, jnp.where(lane >= LANES - 16, here, pltpu.roll(lift, LANES - 16, 1)), lift)
            value = (
                (c0 * here + cw * pltpu.roll(here, 1, 1))
                + (ce * pltpu.roll(here, LANES - 1, 1) + cs * before)
                + (cn * after + vertical_rate * (above + below))
            )
            strips[new, row] = keep(row, value * inside)


def quarter_spec(n):
    return pl.BlockSpec((n, HALO, LEV + STRIP, LANES), lambda i: (i, 0, 0, 0))


STENCIL_SCRATCH = [
    (2, ROWS_Y + 2 * HALO, LEV, LANES),
    (2, ROWS_Y + 2 * HALO, STRIP, LANES),
    (ROWS_Y + 2 * HALO, STRIP, LANES),
]


def coef_specs():
    return [
        whole((5, LEV, LANES)),
        whole((5, STRIP, LANES)),
        pl.BlockSpec(memory_space=pltpu.SMEM),
    ]


def fields_kernel(south, low, high, north, coef, coef_strip, edge, into, out, buf, strips, ends):
    def put(y, at, value):
        out[0, pl.ds(at * ROWS_Y + y, 8, stride=ROWS_Y), :] = value

    substeps(0, (south, low, high, north), coef, coef_strip, edge, buf, strips, ends, put)


def fields(parts, coefs, into):
    n = parts[0].shape[0]
    operands = [*parts, *coefs, into]
    return pl.pallas_call(
        fields_kernel,
        grid=(n,),
        in_specs=[quarter_spec(1) for _ in parts] + coef_specs() + [pl.BlockSpec(memory_space=pltpu.HBM)],
        out_specs=pl.BlockSpec((1, LEV * ROWS_Y, LANES), lambda i: (i + NEAR, 0, 0)),
        out_shape=pltpu.HBM(into.shape, f32),
        scratch_shapes=[pltpu.VMEM(s, f32) for s in STENCIL_SCRATCH],
        input_output_aliases={len(operands) - 1: 0},
        compiler_params=params(),
        name="fields",
    )(*operands)


def gather_kernel(south, low, high, north, coef, coef_strip, edge, counts_in, fields_out, back, *scratch):
    buf, strips, ends, table, counts, out, sems = scratch
    fetch = pltpu.make_async_copy(counts_in, counts, sems.at[0])
    fetch.start()
    save = pltpu.make_async_copy(out, fields_out.at[pl.ds(0, NEAR)], sems.at[1])

    def field(f, carry):
        def put(y, at, value):
            out[f, pl.ds(at * ROWS_Y + y, 8, stride=ROWS_Y), :] = value

        substeps(f, (south, low, high, north), coef, coef_strip, edge, buf, strips, ends, put)
        return carry

    lax.fori_loop(0, NEAR, field, 0)
    save.start()
    for y in range(ROWS_Y):
        cols = slice(y * LANES, (y + 1) * LANES)
        for k in range(NEAR):
            hi, lo = halves(out[k, pl.ds(y, LEV, stride=ROWS_Y), :] * (1.0 / FOOT))
            table[k * LEV : (k + 1) * LEV, cols] = hi
            table[2 * LEV + k * LEV : 2 * LEV + (k + 1) * LEV, cols] = lo
    fetch.wait()
    both = mm(table[...], counts[...], NN)
    sums = both[: 2 * LEV] + both[2 * LEV :]
    for r in range(CAP):
        back[pl.ds(r, DEV, stride=CAP), :] = sums[:, r * DEV : (r + 1) * DEV].T
    save.wait()


def gather(parts, coefs, counts):
    return pl.pallas_call(
        gather_kernel,
        grid=(1,),
        in_specs=[quarter_spec(NEAR) for _ in parts] + coef_specs() + [REMOTE],
        out_specs=[
            REMOTE,
            whole((DEV * CAP, LANES)),
        ],
        out_shape=[
            pltpu.HBM((8, LEV * ROWS_Y, LANES), f32),
            pltpu.HBM((DEV * CAP, LANES), f32),
        ],
        scratch_shapes=[pltpu.VMEM(s, f32) for s in STENCIL_SCRATCH]
        + [
            pltpu.VMEM((4 * LEV, ROWS_Y * LANES), bf16),
            pltpu.VMEM((ROWS_Y * LANES, CAP * DEV), bf16),
            pltpu.VMEM((NEAR, LEV * ROWS_Y, LANES), f32),
            pltpu.SemaphoreType.DMA((2,)),
        ],
        compiler_params=params(),
        name="gather",
    )(*parts, *coefs, counts)


def walls_kernel(inverses, walls, package, product, column, inv_v, wall_v, out, a, b_hi, b_lo, inv_sem, sems, save_sems):
    surfaces, n, _ = wall_v.shape
    first = pltpu.make_async_copy(inverses, inv_v, inv_sem)
    first.start()

    def load(s):
        return pltpu.make_async_copy(walls.at[s], wall_v.at[s], sems.at[s])

    def save(s):
        return pltpu.make_async_copy(out.at[s], product.at[s], save_sems.at[s])

    for s in range(surfaces):
        load(s).start()
    first.wait()

    chosen = jnp.zeros((n, NB), f32)
    for p in range(PKG):
        inv = inv_v[p]
        hi, lo = halves(inv)
        a[:n, p * n : (p + 1) * n] = hi
        a[n:, p * n : (p + 1) * n] = lo
        chosen = jnp.where(package[...] == p, jnp.broadcast_to(inv[:, 0:1], (n, NB)), chosen)
    column[...] = chosen

    def surface(s, carry):
        load(s).wait()
        w = wall_v[s]
        w_hi = w.astype(bf16).astype(f32)
        w_lo = w - w_hi
        for p in range(PKG):
            mine = package[...] == p
            b_hi[p * n : (p + 1) * n, :] = jnp.where(mine, w_hi, 0.0).astype(bf16)
            b_lo[p * n : (p + 1) * n, :] = jnp.where(mine, w_lo, 0.0).astype(bf16)
        both = mm(a[...], b_hi[...], NN)
        out[s] = both[:n] + both[n:] + mm(a[:n, :], b_lo[...], NN)
        save(s).start()
        return carry

    lax.fori_loop(0, surfaces, surface, 0)
    for s in range(surfaces):
        save(s).wait()


def walls_product(inverses, walls, package):
    s, n, _ = walls.shape
    return pl.pallas_call(
        walls_kernel,
        grid=(1,),
        in_specs=[REMOTE, REMOTE, whole((1, NB))],
        out_specs=[REMOTE, whole((n, NB))],
        out_shape=[pltpu.HBM((s, n, NB), f32), pltpu.HBM((n, NB), f32)],
        scratch_shapes=[
            pltpu.VMEM((PKG, n, n), f32),
            pltpu.VMEM((s, n, NB), f32),
            pltpu.VMEM((s, n, NB), f32),
            pltpu.VMEM((2 * n, PKG * n), bf16),
            pltpu.VMEM((PKG * n, NB), bf16),
            pltpu.VMEM((PKG * n, NB), bf16),
            pltpu.SemaphoreType.DMA,
            pltpu.SemaphoreType.DMA((s,)),
            pltpu.SemaphoreType.DMA((s,)),
        ],
        compiler_params=params(),
        name="walls",
    )(inverses, walls, package)


def final_kernel(recv, code_in, facade_in, coeff_in, walls, product, column_in, air_out, walls_out, *scratch):
    xt, code, facade, coeff, first, value, column, load_sems, sems = scratch
    surfaces = value.shape[0]
    pairs = (
        (code_in, code),
        (facade_in, facade),
        (coeff_in, coeff),
        (walls.at[:, pl.ds(0, 8), :], first),
        (product, value),
        (column_in, column),
    )
    loads = [pltpu.make_async_copy(src, dst, load_sems.at[i]) for i, (src, dst) in enumerate(pairs)]
    for c in loads:
        c.start()
    for r in range(CAP):
        hi, lo = halves(recv[pl.ds(r, DEV, stride=CAP), :].T)
        xt[:LANES, r * DEV : (r + 1) * DEV] = hi
        xt[LANES:, r * DEV : (r + 1) * DEV] = lo
    loads[0].wait()
    picks = []
    for r in range(CAP):
        picks.append(jnp.where(code[...] == float(r), 1.0, 0.0).astype(bf16))
    both = mm(xt[...], jnp.concatenate(picks, axis=0), NN)
    air = both[:LANES] + both[LANES:]
    air_out[...] = air
    for c in loads[1:]:
        c.wait()
    area = facade[...]
    temp = jnp.sum(area * air[:LEV], axis=0, keepdims=True) / jnp.sum(area, axis=0, keepdims=True)
    saves = []
    for s in range(surfaces):
        source = wall_gain * coeff[s : s + 1, :] * (temp - first[s, 0:1, :])
        value[s] = value[s] + column[...] * source
        saves.append(pltpu.make_async_copy(value.at[s], walls_out.at[s], sems.at[s]))
        saves[s].start()
    for c in saves:
        c.wait()


def final(recv, code, facade, coeff, walls, product, column):
    s, n, _ = walls.shape
    return pl.pallas_call(
        final_kernel,
        grid=(1,),
        in_specs=[
            whole((DEV * CAP, LANES)),
            REMOTE,
            REMOTE,
            REMOTE,
            REMOTE,
            REMOTE,
            REMOTE,
        ],
        out_specs=[whole((2 * LEV, NB)), REMOTE],
        out_shape=[
            jax.ShapeDtypeStruct((2 * LEV, NB), f32),
            pltpu.HBM((s, n, NB), f32),
        ],
        scratch_shapes=[
            pltpu.VMEM((2 * LANES, CAP * DEV), bf16),
            pltpu.VMEM((DEV, NB), f32),
            pltpu.VMEM((LEV, NB), f32),
            pltpu.VMEM((s, NB), f32),
            pltpu.VMEM((s, 8, NB), f32),
            pltpu.VMEM((s, n, NB), f32),
            pltpu.VMEM((n, NB), f32),
            pltpu.SemaphoreType.DMA((6,)),
            pltpu.SemaphoreType.DMA((s,)),
        ],
        compiler_params=params(),
        name="final",
    )(recv, code, facade, coeff, walls, product, column)


def transpose_all(x, rows):
    y = lax.all_to_all(
        x.reshape(DEV, 1, rows * LANES), ("gx", "gy"), split_axis=0, concat_axis=0, tiled=True
    )
    return y.reshape(DEV * rows, LANES)


def inside_edges():
    gx, gy = lax.axis_index("gx"), lax.axis_index("gy")
    side = jnp.arange(4, dtype=jnp.int32)
    place = jnp.where(side < 2, gy, gx)
    limit = jnp.where(side < 2, lax.axis_size("gy") - 1, lax.axis_size("gx") - 1)
    return jnp.where(side % 2 == 0, place > 0, place < limit).astype(f32)


def hbm(x):
    return pltpu.with_memory_space_constraint(x, pltpu.HBM)


def body(canopy, courant, walls, inverses, package, surf_coeff, facade_area, anchor, footprint):
    shape = canopy.shape
    canopy = canopy.reshape(shape[0], LEV * ROWS_Y, LANES)
    edge = inside_edges()
    send, code = payload(hbm(anchor.T), hbm(footprint.T), hbm(surf_coeff), hbm(walls), hbm(facade_area))
    recv = transpose_all(send, FLUX_ROWS)
    later, code = lax.optimization_barrier((canopy, code))
    low, high, pack, coef, coef_strip = prep(hbm(courant), hbm(later))
    coefs = (hbm(coef), hbm(coef_strip), edge)
    low, high, _ = across_x(low, high, pack)
    recv, low, high = lax.optimization_barrier((recv, low, high))
    up, down = shifts("gy")
    south = lax.ppermute(high, "gy", up)
    counts, near_low, near_high, pack = scatter(recv, hbm(canopy))
    near_low, near_high, _ = across_x(near_low, near_high, pack)
    near_low, near_high, low, walls_later = lax.optimization_barrier((near_low, near_high, low, walls))
    near = across_y(near_low, near_high)
    north = lax.ppermute(low, "gy", down)
    product, column = walls_product(hbm(inverses), hbm(walls_later), hbm(package[None, :]))
    near, south, product = lax.optimization_barrier((near, south, product))
    rest = (south, low, high, north)
    out, back = gather(near, coefs, hbm(counts))
    returned = transpose_all(back, CAP)
    out = fields(rest, coefs, out)
    air, walls_out = final(returned, hbm(code), hbm(facade_area), hbm(surf_coeff), hbm(walls), hbm(product), hbm(column))
    return out.reshape(shape), air.reshape(2, LEV, NB), walls_out


def solution(mesh):
    placed = (
        P(None, None, "gy", "gx"),
        P(),
        P(None, None, ("gx", "gy")),
        P(),
        P(("gx", "gy")),
        P(None, ("gx", "gy")),
        P(None, ("gx", "gy")),
        P(("gx", "gy"), None),
        P(("gx", "gy"), None),
    )
    return jax.shard_map(
        body,
        mesh=mesh,
        in_specs=placed,
        out_specs=(
            P(None, None, "gy", "gx"),
            P(None, None, ("gx", "gy")),
            P(None, None, ("gx", "gy")),
        ),
        check_vma=False,
    )
```

```python
import functools

import jax
import jax.numpy as jnp
from jax import lax
from jax.experimental import pallas as pl
from jax.experimental.pallas import tpu as pltpu
from jax.sharding import PartitionSpec as P

PKG = 8
SUB = 4
HALO = 4
CAP = 10
FOOT = 8
DEV = 128
LEV = 64
NB = 256
ROWS_Y = 8
LANES = 128
FLUX_ROWS = 6
STRIP = 8
AUX = 2 + FOOT
NEAR = 2

source_rate = 0.1
kappa_rate = 0.05
vertical_rate = 0.05
wall_gain = 0.5

f32 = jnp.float32
bf16 = jnp.bfloat16
VMEM = 16 * 1024 * 1024
NT = (((1,), (1,)), ((), ()))
NN = (((1,), (0,)), ((), ()))


def params(**kw):
    return pltpu.CompilerParams(vmem_limit_bytes=VMEM, **kw)


def whole(shape):
    return pl.BlockSpec(shape, lambda *_: (0,) * len(shape))


REMOTE = pl.BlockSpec(memory_space=pltpu.HBM)


def halves(x):
    hi = x.astype(bf16)
    lo = (x - hi.astype(f32)).astype(bf16)
    return hi, lo


def mm(a, b, dims):
    return lax.dot_general(a, b, dims, preferred_element_type=f32)


def payload_kernel(anchor, foot, coeff, walls, facade, out, code_out, aux):
    owner = lax.broadcasted_iota(jnp.int32, (DEV, NB), 0) == anchor[...]
    earlier = lax.broadcasted_iota(jnp.int32, (NB, NB), 0) < lax.broadcasted_iota(
        jnp.int32, (NB, NB), 1
    )
    rank = mm(jnp.where(owner, 1.0, 0.0).astype(bf16), jnp.where(earlier, 1.0, 0.0).astype(bf16), NN)
    code = jnp.where(owner, rank, -1.0)
    code_out[...] = code
    heat = jnp.sum(coeff[...] * walls[:, 0, :], axis=0, keepdims=True)
    coupling = jnp.sum(coeff[...], axis=0, keepdims=True)
    cells = foot[...].astype(f32)
    picks = [jnp.where(code == float(r), 1.0, 0.0).astype(bf16) for r in range(CAP)]
    hi, lo = halves(facade[...])
    zero = jnp.zeros((LEV, NB), bf16)
    even = jnp.concatenate([picks[2 * p] for p in range(CAP // 2)], axis=0)
    odd = jnp.concatenate([picks[2 * p + 1] for p in range(CAP // 2)], axis=0)
    rows = (
        mm(even, jnp.concatenate([hi, zero], axis=0), NT)
        + mm(odd, jnp.concatenate([zero, hi], axis=0), NT)
        + mm(even, jnp.concatenate([lo, zero], axis=0), NT)
        + mm(odd, jnp.concatenate([zero, lo], axis=0), NT)
    )
    for p in range(CAP // 2):
        out[pl.ds(p, DEV, stride=FLUX_ROWS), :] = rows[p * DEV : (p + 1) * DEV]
    aux[...] = jnp.zeros_like(aux)
    for r in range(CAP):
        aux[r, AUX * r : AUX * r + 1, :] = heat
        aux[r, AUX * r + 1 : AUX * r + 2, :] = coupling
        aux[r, AUX * r + 2 : AUX * r + AUX, :] = cells
    total = jnp.zeros((DEV, LANES), f32)
    for r in range(CAP):
        hi, lo = halves(aux[r])
        total = total + mm(picks[r], hi, NT) + mm(picks[r], lo, NT)
    out[pl.ds(CAP // 2, DEV, stride=FLUX_ROWS), :] = total


def payload(anchor, foot, coeff, walls, facade):
    return pl.pallas_call(
        payload_kernel,
        grid=(1,),
        in_specs=[
            whole((1, NB)),
            whole((FOOT, NB)),
            whole((6, NB)),
            pl.BlockSpec((6, 8, NB), lambda _: (0, 0, 0)),
            whole((LEV, NB)),
        ],
        out_specs=[whole((DEV * FLUX_ROWS, LANES)), whole((DEV, NB))],
        out_shape=[
            pltpu.HBM((DEV * FLUX_ROWS, LANES), f32),
            pltpu.HBM((DEV, NB), f32),
        ],
        scratch_shapes=[pltpu.VMEM((CAP, LANES, NB), f32)],
        compiler_params=params(),
        name="payload",
    )(anchor, foot, coeff, walls, facade)


def lane_slot():
    return lax.broadcasted_iota(jnp.int32, (8, LANES), 1)


def pack_row(blocks):
    lane = lane_slot()
    slot = lane % 16
    out = jnp.zeros((8, LANES), f32)
    for i, block in enumerate(blocks):
        here = lane // 16 == i
        west = here & (slot >= 4) & (slot < 8)
        east = here & (slot >= 8) & (slot < 12)
        out = jnp.where(west, pltpu.roll(block, (16 * i + 4) % LANES, 1), out)
        out = jnp.where(east, pltpu.roll(block, (16 * i + 12) % LANES, 1), out)
    return out


def emit_row(f, y, field, low, high, pack):
    dst = low if y < HALO else high
    dst[f, y % HALO, :LEV, :] = field
    row = pack_row([field[8 * i : 8 * i + 8] for i in range(8)])
    if y < HALO:
        pack[f, y] = row
    else:
        pack[f, y - HALO] = pack[f, y - HALO] + pltpu.roll(row, 8, 1)


def prep_kernel(courant_in, canopy, low, high, pack, coef, coef_strip, field, courant, sems):
    n = field.shape[0]
    loads = [pltpu.make_async_copy(canopy.at[NEAR + f], field.at[f], sems.at[f]) for f in range(n)]
    given = pltpu.make_async_copy(courant_in, courant, sems.at[n])
    given.start()
    for c in loads:
        c.start()
    given.wait()
    square = (LEV, LEV)
    diagonal = lax.broadcasted_iota(jnp.int32, square, 0) == lax.broadcasted_iota(jnp.int32, square, 1)

    def column(row):
        picked = jnp.where(diagonal, jnp.broadcast_to(courant[row : row + 1, :], square), 0.0)
        return jnp.broadcast_to(jnp.sum(picked, axis=1, keepdims=True), (LEV, LANES))

    cx, cy = column(0), column(1)
    values = (
        1.0 - jnp.abs(cx) - jnp.abs(cy) - (4.0 * kappa_rate + 2.0 * vertical_rate),
        jnp.maximum(cx, 0.0) + kappa_rate,
        kappa_rate - jnp.minimum(cx, 0.0),
        jnp.maximum(cy, 0.0) + kappa_rate,
        kappa_rate - jnp.minimum(cy, 0.0),
    )
    block = lane_slot() // 16
    for k, v in enumerate(values):
        coef[k] = v
        strip = v[0:8]
        for i in range(1, 8):
            strip = jnp.where(block == i, v[8 * i : 8 * i + 8], strip)
        coef_strip[k] = strip
    for f in range(n):
        loads[f].wait()
        for y in range(ROWS_Y):
            emit_row(f, y, field[f, pl.ds(y, LEV, stride=ROWS_Y), :], low, high, pack)


def half_shape(n):
    return jax.ShapeDtypeStruct((n, HALO, LEV + STRIP, LANES), f32)


def pack_shape(n):
    return jax.ShapeDtypeStruct((n, HALO, STRIP, LANES), f32)


def half_spec(n):
    return pl.BlockSpec((n, HALO, LEV, LANES), lambda i: (0, 0, 0, 0))


def prep(courant, canopy):
    n = canopy.shape[0] - NEAR
    return pl.pallas_call(
        prep_kernel,
        grid=(1,),
        in_specs=[REMOTE, REMOTE],
        out_specs=[
            half_spec(n),
            half_spec(n),
            whole((n, HALO, STRIP, LANES)),
            whole((5, LEV, LANES)),
            whole((5, STRIP, LANES)),
        ],
        out_shape=[
            half_shape(n),
            half_shape(n),
            pack_shape(n),
            pltpu.HBM((5, LEV, LANES), f32),
            pltpu.HBM((5, STRIP, LANES), f32),
        ],
        scratch_shapes=[
            pltpu.VMEM((n, LEV * ROWS_Y, LANES), f32),
            pltpu.VMEM((2, LEV), f32),
            pltpu.SemaphoreType.DMA((n + 1,)),
        ],
        compiler_params=params(),
        name="prep",
    )(courant, canopy)


def scatter_kernel(recv, canopy, counts_out, low, high, pack, counts, column_s, field_s, xt, near, sems):
    load = pltpu.make_async_copy(canopy.at[pl.ds(0, NEAR)], near, sems.at[0])
    load.start()
    aux = recv[pl.ds(CAP // 2, DEV, stride=FLUX_ROWS), :].T
    cell = aux.astype(jnp.int32)
    column_s[...] = cell & (LANES - 1)
    field_s[...] = lax.shift_left(jnp.ones_like(cell), lax.shift_right_logical(cell, jnp.full_like(cell, 5)) & 28)

    def group(g, carry):
        start = pl.multiple_of(g * 16, 16)
        x = lax.broadcasted_iota(jnp.int32, (16, LANES), 0) + start
        for r in range(CAP):
            packed = jnp.zeros((16, LANES), jnp.int32)
            for k in range(AUX * r + 2, AUX * r + AUX):
                here = jnp.broadcast_to(column_s[k : k + 1, :], (16, LANES)) == x
                packed = packed + jnp.where(here, jnp.broadcast_to(field_s[k : k + 1, :], (16, LANES)), 0)
            for y in range(ROWS_Y):
                n = lax.shift_right_logical(packed, jnp.full_like(packed, 4 * y)) & 15
                row = pl.multiple_of(y * LANES + start, 16)
                counts[pl.ds(row, 16), r * DEV : (r + 1) * DEV] = n.astype(f32).astype(bf16)
        return carry

    lax.fori_loop(0, LANES // 16, group, 0)
    save = pltpu.make_async_copy(counts, counts_out, sems.at[1])
    save.start()
    for p in range(CAP // 2):
        rows = recv[pl.ds(p, DEV, stride=FLUX_ROWS), :].T
        for odd in range(2):
            r = 2 * p + odd
            area = rows[LEV * odd : LEV * (odd + 1)]
            for q in range(2):
                hi, lo = halves(area * aux[AUX * r + q : AUX * r + q + 1, :])
                xt[q * LEV : (q + 1) * LEV, r * DEV : (r + 1) * DEV] = hi
                xt[DEV + q * LEV : DEV + (q + 1) * LEV, r * DEV : (r + 1) * DEV] = lo
    both = mm(xt[...], counts[...], NT)
    sums = both[:DEV] + both[DEV:]
    load.wait()
    for y in range(ROWS_Y):
        c = near[0, pl.ds(y, LEV, stride=ROWS_Y), :]
        p = sums[:LEV, y * LANES : (y + 1) * LANES]
        q = sums[LEV:, y * LANES : (y + 1) * LANES]
        emit_row(0, y, c + (source_rate / FOOT) * (p - q * c), low, high, pack)
        for f in range(1, NEAR):
            emit_row(f, y, near[f, pl.ds(y, LEV, stride=ROWS_Y), :], low, high, pack)
    save.wait()


def scatter(recv, canopy):
    return pl.pallas_call(
        scatter_kernel,
        grid=(1,),
        in_specs=[whole((DEV * FLUX_ROWS, LANES)), pl.BlockSpec(memory_space=pltpu.HBM)],
        out_specs=[
            REMOTE,
            half_spec(NEAR),
            half_spec(NEAR),
            whole((NEAR, HALO, STRIP, LANES)),
        ],
        out_shape=[
            pltpu.HBM((ROWS_Y * LANES, CAP * DEV), bf16),
            half_shape(NEAR),
            half_shape(NEAR),
            pack_shape(NEAR),
        ],
        scratch_shapes=[
            pltpu.VMEM((ROWS_Y * LANES, CAP * DEV), bf16),
            pltpu.VMEM((LANES, DEV), jnp.int32),
            pltpu.VMEM((LANES, DEV), jnp.int32),
            pltpu.VMEM((2 * DEV, CAP * DEV), bf16),
            pltpu.VMEM((NEAR, LEV * ROWS_Y, LANES), f32),
            pltpu.SemaphoreType.DMA((2,)),
        ],
        compiler_params=params(),
        name="scatter",
    )(recv, canopy)


def merge_kernel(pack, west, east, low_in, high_in, low, high):
    slot = lane_slot() % 16
    for f in range(pack.shape[0]):
        for y in range(ROWS_Y):
            w, own, e = west[f, y % HALO], pack[f, y % HALO], east[f, y % HALO]
            if y < HALO:
                w, e = pltpu.roll(w, LANES - 8, 1), pltpu.roll(e, 8, 1)
            else:
                w, own = pltpu.roll(w, LANES - 16, 1), pltpu.roll(own, LANES - 8, 1)
            dst = low if y < HALO else high
            dst[f, y % HALO] = jnp.where(slot < 4, w, jnp.where(slot < 12, own, e))


def merge(pack, west, east, low, high):
    n = pack.shape[0]
    pack_spec = whole((n, HALO, STRIP, LANES))
    strip_spec = pl.BlockSpec((n, HALO, STRIP, LANES), lambda i: (0, 0, LEV // STRIP, 0))
    anywhere = pl.BlockSpec(memory_space=pl.ANY)
    return pl.pallas_call(
        merge_kernel,
        grid=(1,),
        in_specs=[pack_spec, pack_spec, pack_spec, anywhere, anywhere],
        out_specs=[strip_spec, strip_spec],
        out_shape=[half_shape(n), half_shape(n)],
        input_output_aliases={3: 0, 4: 1},
        compiler_params=params(),
        name="merge",
    )(pack, west, east, low, high)


def shifts(axis):
    up = [(i, i + 1) for i in range(lax.axis_size(axis) - 1)]
    return up, [(j, i) for i, j in up]


def across_x(low, high, pack, beside=None):
    up, down = shifts("gx")
    west, east = lax.ppermute(pack, "gx", up), lax.ppermute(pack, "gx", down)
    done = None
    if beside is not None:
        done = beside()
        west, east, done = lax.optimization_barrier((west, east, done))
    low, high = merge(pack, west, east, low, high)
    return low, high, done


def across_y(low, high):
    up, down = shifts("gy")
    south, north = lax.ppermute(high, "gy", up), lax.ppermute(low, "gy", down)
    return south, low, high, north


def substeps(f, parts, coef, coef_strip, edge, buf, strips, ends, put):
    lane = lane_slot()
    sub = lax.broadcasted_iota(jnp.int32, (8, LANES), 0)
    slot = lane % 16
    first, last = lane == 0, lane == LANES - 1
    inside = jnp.where(slot < 4, edge[2], jnp.where(slot < 12, 1.0, edge[3]))
    total = ROWS_Y + 2 * HALO

    def keep(row, value):
        if row < HALO:
            return value * edge[0]
        if row >= HALO + ROWS_Y:
            return value * edge[1]
        return value

    for step in range(1, SUB + 1):
        old, new = (step + 1) % 2, step % 2

        def main(row, start):
            if step == 1:
                return parts[row // HALO][f, row % HALO, start : start + 8, :]
            return buf[old, row, start : start + 8, :]

        def strip(row):
            if step == 1:
                return parts[row // HALO][f, row % HALO, LEV : LEV + STRIP, :]
            return strips[old, row]

        rows = range(step, total - step)
        for row in rows:
            side = strip(row)
            ends[row] = jnp.where(slot == 3, side, pltpu.roll(side, LANES - 10, 1))
        for i in range(8):
            at = 8 * i
            c0, cw, ce, cs, cn = (coef[k, at : at + 8, :] for k in range(5))
            here, after = main(step - 1, at), main(step, at)
            for row in rows:
                before, here, after = here, after, main(row + 1, at)
                if i == 0:
                    below = jnp.where(sub == 0, here, pltpu.roll(here, 1, 0))
                else:
                    below = pltpu.roll(jnp.where(sub == 7, main(row, at - 8), here), 1, 0)
                if i == 7:
                    above = jnp.where(sub == 7, here, pltpu.roll(here, 7, 0))
                else:
                    above = pltpu.roll(jnp.where(sub == 0, main(row, at + 8), here), 7, 0)
                side = pltpu.roll(ends[row], (LANES - 16 * i - 3) % LANES, 1)
                left = jnp.where(first, side, pltpu.roll(here, 1, 1))
                right = jnp.where(last, side, pltpu.roll(here, LANES - 1, 1))
                value = (
                    (c0 * here + cw * left)
                    + (ce * right + cs * before)
                    + (cn * after + vertical_rate * (above + below))
                )
                if step == SUB:
                    put(row - HALO, at, value)
                else:
                    buf[new, row, at : at + 8, :] = keep(row, value)
        if step == SUB:
            break
        c0, cw, ce, cs, cn = (coef_strip[k] for k in range(5))
        here, after = strip(step - 1), strip(step)
        for row in rows:
            before, here, after = here, after, strip(row + 1)
            down = pltpu.roll(here, 1, 0)
            below = jnp.where(sub == 0, jnp.where(lane < 16, here, pltpu.roll(down, 16, 1)), down)
            lift = pltpu.roll(here, 7, 0)
            above = jnp.where(sub == 7, jnp.where(lane >= LANES - 16, here, pltpu.roll(lift, LANES - 16, 1)), lift)
            value = (
                (c0 * here + cw * pltpu.roll(here, 1, 1))
                + (ce * pltpu.roll(here, LANES - 1, 1) + cs * before)
                + (cn * after + vertical_rate * (above + below))
            )
            strips[new, row] = keep(row, value * inside)


def quarter_spec(n):
    return pl.BlockSpec((n, HALO, LEV + STRIP, LANES), lambda i: (i, 0, 0, 0))


STENCIL_SCRATCH = [
    (2, ROWS_Y + 2 * HALO, LEV, LANES),
    (2, ROWS_Y + 2 * HALO, STRIP, LANES),
    (ROWS_Y + 2 * HALO, STRIP, LANES),
]


def coef_specs():
    return [
        whole((5, LEV, LANES)),
        whole((5, STRIP, LANES)),
        pl.BlockSpec(memory_space=pltpu.SMEM),
    ]


def fields_kernel(south, low, high, north, coef, coef_strip, edge, into, out, buf, strips, ends):
    def put(y, at, value):
        out[0, pl.ds(at * ROWS_Y + y, 8, stride=ROWS_Y), :] = value

    substeps(0, (south, low, high, north), coef, coef_strip, edge, buf, strips, ends, put)


def fields(parts, coefs, into):
    n = parts[0].shape[0]
    operands = [*parts, *coefs, into]
    return pl.pallas_call(
        fields_kernel,
        grid=(n,),
        in_specs=[quarter_spec(1) for _ in parts] + coef_specs() + [pl.BlockSpec(memory_space=pltpu.HBM)],
        out_specs=pl.BlockSpec((1, LEV * ROWS_Y, LANES), lambda i: (i + NEAR, 0, 0)),
        out_shape=pltpu.HBM(into.shape, f32),
        scratch_shapes=[pltpu.VMEM(s, f32) for s in STENCIL_SCRATCH],
        input_output_aliases={len(operands) - 1: 0},
        compiler_params=params(),
        name="fields",
    )(*operands)


def gather_kernel(south, low, high, north, coef, coef_strip, edge, counts_in, fields_out, back, *scratch):
    buf, strips, ends, table, counts, out, sems = scratch
    fetch = pltpu.make_async_copy(counts_in, counts, sems.at[0])
    fetch.start()
    save = pltpu.make_async_copy(out, fields_out.at[pl.ds(0, NEAR)], sems.at[1])

    def field(f, carry):
        def put(y, at, value):
            out[f, pl.ds(at * ROWS_Y + y, 8, stride=ROWS_Y), :] = value

        substeps(f, (south, low, high, north), coef, coef_strip, edge, buf, strips, ends, put)
        return carry

    lax.fori_loop(0, NEAR, field, 0)
    save.start()
    for y in range(ROWS_Y):
        cols = slice(y * LANES, (y + 1) * LANES)
        for k in range(NEAR):
            hi, lo = halves(out[k, pl.ds(y, LEV, stride=ROWS_Y), :] * (1.0 / FOOT))
            table[k * LEV : (k + 1) * LEV, cols] = hi
            table[2 * LEV + k * LEV : 2 * LEV + (k + 1) * LEV, cols] = lo
    fetch.wait()
    both = mm(table[...], counts[...], NN)
    sums = both[: 2 * LEV] + both[2 * LEV :]
    for r in range(CAP):
        back[pl.ds(r, DEV, stride=CAP), :] = sums[:, r * DEV : (r + 1) * DEV].T
    save.wait()


def gather(parts, coefs, counts):
    return pl.pallas_call(
        gather_kernel,
        grid=(1,),
        in_specs=[quarter_spec(NEAR) for _ in parts] + coef_specs() + [REMOTE],
        out_specs=[
            REMOTE,
            whole((DEV * CAP, LANES)),
        ],
        out_shape=[
            pltpu.HBM((8, LEV * ROWS_Y, LANES), f32),
            pltpu.HBM((DEV * CAP, LANES), f32),
        ],
        scratch_shapes=[pltpu.VMEM(s, f32) for s in STENCIL_SCRATCH]
        + [
            pltpu.VMEM((4 * LEV, ROWS_Y * LANES), bf16),
            pltpu.VMEM((ROWS_Y * LANES, CAP * DEV), bf16),
            pltpu.VMEM((NEAR, LEV * ROWS_Y, LANES), f32),
            pltpu.SemaphoreType.DMA((2,)),
        ],
        compiler_params=params(),
        name="gather",
    )(*parts, *coefs, counts)


def walls_kernel(inverses, walls, package, product, column, inv_v, wall_v, out, a, b_hi, b_lo, inv_sem, sems, save_sems):
    surfaces, n, _ = wall_v.shape
    first = pltpu.make_async_copy(inverses, inv_v, inv_sem)
    first.start()

    def load(s):
        return pltpu.make_async_copy(walls.at[s], wall_v.at[s], sems.at[s])

    def save(s):
        return pltpu.make_async_copy(out.at[s], product.at[s], save_sems.at[s])

    for s in range(surfaces):
        load(s).start()
    first.wait()

    chosen = jnp.zeros((n, NB), f32)
    for p in range(PKG):
        inv = inv_v[p]
        hi, lo = halves(inv)
        a[:n, p * n : (p + 1) * n] = hi
        a[n:, p * n : (p + 1) * n] = lo
        chosen = jnp.where(package[...] == p, jnp.broadcast_to(inv[:, 0:1], (n, NB)), chosen)
    column[...] = chosen

    masks = [jnp.where(package[...] == p, 1.0, 0.0) for p in range(PKG)]

    def surface(s, carry):
        load(s).wait()
        w_hi, w_lo = halves(wall_v[s])
        for p in range(PKG):
            mine = jnp.broadcast_to(masks[p], (n, NB)).astype(bf16)
            b_hi[p * n : (p + 1) * n, :] = w_hi * mine
            b_lo[p * n : (p + 1) * n, :] = w_lo * mine
        both = mm(a[...], b_hi[...], NN)
        out[s] = both[:n] + both[n:] + mm(a[:n, :], b_lo[...], NN)
        save(s).start()
        return carry

    lax.fori_loop(0, surfaces, surface, 0)
    for s in range(surfaces):
        save(s).wait()


def walls_product(inverses, walls, package):
    s, n, _ = walls.shape
    return pl.pallas_call(
        walls_kernel,
        grid=(1,),
        in_specs=[REMOTE, REMOTE, whole((1, NB))],
        out_specs=[REMOTE, whole((n, NB))],
        out_shape=[pltpu.HBM((s, n, NB), f32), pltpu.HBM((n, NB), f32)],
        scratch_shapes=[
            pltpu.VMEM((PKG, n, n), f32),
            pltpu.VMEM((s, n, NB), f32),
            pltpu.VMEM((s, n, NB), f32),
            pltpu.VMEM((2 * n, PKG * n), bf16),
            pltpu.VMEM((PKG * n, NB), bf16),
            pltpu.VMEM((PKG * n, NB), bf16),
            pltpu.SemaphoreType.DMA,
            pltpu.SemaphoreType.DMA((s,)),
            pltpu.SemaphoreType.DMA((s,)),
        ],
        compiler_params=params(),
        name="walls",
    )(inverses, walls, package)


def final_kernel(recv, code_in, facade_in, coeff_in, walls, product, column_in, air_out, walls_out, *scratch):
    xt, code, facade, coeff, first, value, column, load_sems, sems = scratch
    surfaces = value.shape[0]
    pairs = (
        (code_in, code),
        (facade_in, facade),
        (coeff_in, coeff),
        (walls.at[:, pl.ds(0, 8), :], first),
        (product, value),
        (column_in, column),
    )
    loads = [pltpu.make_async_copy(src, dst, load_sems.at[i]) for i, (src, dst) in enumerate(pairs)]
    for c in loads:
        c.start()
    for r in range(CAP):
        hi, lo = halves(recv[pl.ds(r, DEV, stride=CAP), :].T)
        xt[:LANES, r * DEV : (r + 1) * DEV] = hi
        xt[LANES:, r * DEV : (r + 1) * DEV] = lo
    loads[0].wait()
    picks = []
    for r in range(CAP):
        picks.append(jnp.where(code[...] == float(r), 1.0, 0.0).astype(bf16))
    both = mm(xt[...], jnp.concatenate(picks, axis=0), NN)
    air = both[:LANES] + both[LANES:]
    air_out[...] = air
    for c in loads[1:]:
        c.wait()
    area = facade[...]
    temp = jnp.sum(area * air[:LEV], axis=0, keepdims=True) / jnp.sum(area, axis=0, keepdims=True)
    saves = []
    for s in range(surfaces):
        source = wall_gain * coeff[s : s + 1, :] * (temp - first[s, 0:1, :])
        value[s] = value[s] + column[...] * source
        saves.append(pltpu.make_async_copy(value.at[s], walls_out.at[s], sems.at[s]))
        saves[s].start()
    for c in saves:
        c.wait()


def final(recv, code, facade, coeff, walls, product, column):
    s, n, _ = walls.shape
    return pl.pallas_call(
        final_kernel,
        grid=(1,),
        in_specs=[
            whole((DEV * CAP, LANES)),
            REMOTE,
            REMOTE,
            REMOTE,
            REMOTE,
            REMOTE,
            REMOTE,
        ],
        out_specs=[whole((2 * LEV, NB)), REMOTE],
        out_shape=[
            jax.ShapeDtypeStruct((2 * LEV, NB), f32),
            pltpu.HBM((s, n, NB), f32),
        ],
        scratch_shapes=[
            pltpu.VMEM((2 * LANES, CAP * DEV), bf16),
            pltpu.VMEM((DEV, NB), f32),
            pltpu.VMEM((LEV, NB), f32),
            pltpu.VMEM((s, NB), f32),
            pltpu.VMEM((s, 8, NB), f32),
            pltpu.VMEM((s, n, NB), f32),
            pltpu.VMEM((n, NB), f32),
            pltpu.SemaphoreType.DMA((6,)),
            pltpu.SemaphoreType.DMA((s,)),
        ],
        compiler_params=params(),
        name="final",
    )(recv, code, facade, coeff, walls, product, column)


def transpose_all(x, rows):
    y = lax.all_to_all(
        x.reshape(DEV, 1, rows * LANES), ("gx", "gy"), split_axis=0, concat_axis=0, tiled=True
    )
    return y.reshape(DEV * rows, LANES)


def inside_edges():
    gx, gy = lax.axis_index("gx"), lax.axis_index("gy")
    side = jnp.arange(4, dtype=jnp.int32)
    place = jnp.where(side < 2, gy, gx)
    limit = jnp.where(side < 2, lax.axis_size("gy") - 1, lax.axis_size("gx") - 1)
    return jnp.where(side % 2 == 0, place > 0, place < limit).astype(f32)


def hbm(x):
    return pltpu.with_memory_space_constraint(x, pltpu.HBM)


def body(canopy, courant, walls, inverses, package, surf_coeff, facade_area, anchor, footprint):
    shape = canopy.shape
    canopy = canopy.reshape(shape[0], LEV * ROWS_Y, LANES)
    edge = inside_edges()
    send, code = payload(hbm(anchor.T), hbm(footprint.T), hbm(surf_coeff), hbm(walls), hbm(facade_area))
    recv = transpose_all(send, FLUX_ROWS)
    later, code = lax.optimization_barrier((canopy, code))
    low, high, pack, coef, coef_strip = prep(hbm(courant), hbm(later))
    coefs = (hbm(coef), hbm(coef_strip), edge)
    low, high, _ = across_x(low, high, pack)
    recv, low, high = lax.optimization_barrier((recv, low, high))
    up, down = shifts("gy")
    south = lax.ppermute(high, "gy", up)
    counts, near_low, near_high, pack = scatter(recv, hbm(canopy))
    near_low, near_high, _ = across_x(near_low, near_high, pack)
    near_low, near_high, low, walls_later = lax.optimization_barrier((near_low, near_high, low, walls))
    near = across_y(near_low, near_high)
    north = lax.ppermute(low, "gy", down)
    product, column = walls_product(hbm(inverses), hbm(walls_later), hbm(package[None, :]))
    near, south, product = lax.optimization_barrier((near, south, product))
    rest = (south, low, high, north)
    out, back = gather(near, coefs, hbm(counts))
    returned = transpose_all(back, CAP)
    out = fields(rest, coefs, out)
    air, walls_out = final(returned, hbm(code), hbm(facade_area), hbm(surf_coeff), hbm(walls), hbm(product), hbm(column))
    return out.reshape(shape), air.reshape(2, LEV, NB), walls_out


def solution(mesh):
    placed = (
        P(None, None, "gy", "gx"),
        P(),
        P(None, None, ("gx", "gy")),
        P(),
        P(("gx", "gy")),
        P(None, ("gx", "gy")),
        P(None, ("gx", "gy")),
        P(("gx", "gy"), None),
        P(("gx", "gy"), None),
    )
    return jax.shard_map(
        body,
        mesh=mesh,
        in_specs=placed,
        out_specs=(
            P(None, None, "gy", "gx"),
            P(None, None, ("gx", "gy")),
            P(None, None, ("gx", "gy")),
        ),
        check_vma=False,
    )
```

```python
import functools

import jax
import jax.numpy as jnp
from jax import lax
from jax.experimental import pallas as pl
from jax.experimental.pallas import tpu as pltpu
from jax.sharding import PartitionSpec as P

PKG = 8
SUB = 4
HALO = 4
CAP = 10
FOOT = 8
DEV = 128
LEV = 64
NB = 256
ROWS_Y = 8
LANES = 128
FLUX_ROWS = 6
STRIP = 8
AUX = 2 + FOOT
NEAR = 2

source_rate = 0.1
kappa_rate = 0.05
vertical_rate = 0.05
wall_gain = 0.5

f32 = jnp.float32
bf16 = jnp.bfloat16
VMEM = 16 * 1024 * 1024
NT = (((1,), (1,)), ((), ()))
NN = (((1,), (0,)), ((), ()))


def params(**kw):
    return pltpu.CompilerParams(vmem_limit_bytes=VMEM, **kw)


def whole(shape):
    return pl.BlockSpec(shape, lambda *_: (0,) * len(shape))


REMOTE = pl.BlockSpec(memory_space=pltpu.HBM)


def halves(x):
    hi = x.astype(bf16)
    lo = (x - hi.astype(f32)).astype(bf16)
    return hi, lo


def mm(a, b, dims):
    return lax.dot_general(a, b, dims, preferred_element_type=f32)


def payload_kernel(anchor, foot, coeff, walls, facade, out, code_out, aux):
    owner = lax.broadcasted_iota(jnp.int32, (DEV, NB), 0) == anchor[...]
    earlier = lax.broadcasted_iota(jnp.int32, (NB, NB), 0) < lax.broadcasted_iota(
        jnp.int32, (NB, NB), 1
    )
    rank = mm(jnp.where(owner, 1.0, 0.0).astype(bf16), jnp.where(earlier, 1.0, 0.0).astype(bf16), NN)
    code = jnp.where(owner, rank, -1.0)
    code_out[...] = code
    heat = jnp.sum(coeff[...] * walls[:, 0, :], axis=0, keepdims=True)
    coupling = jnp.sum(coeff[...], axis=0, keepdims=True)
    cells = foot[...].astype(f32)
    picks = [jnp.where(code == float(r), 1.0, 0.0).astype(bf16) for r in range(CAP)]
    hi, lo = halves(facade[...])
    zero = jnp.zeros((LEV, NB), bf16)
    even = jnp.concatenate([picks[2 * p] for p in range(CAP // 2)], axis=0)
    odd = jnp.concatenate([picks[2 * p + 1] for p in range(CAP // 2)], axis=0)
    rows = (
        mm(even, jnp.concatenate([hi, zero], axis=0), NT)
        + mm(odd, jnp.concatenate([zero, hi], axis=0), NT)
        + mm(even, jnp.concatenate([lo, zero], axis=0), NT)
        + mm(odd, jnp.concatenate([zero, lo], axis=0), NT)
    )
    for p in range(CAP // 2):
        out[pl.ds(p, DEV, stride=FLUX_ROWS), :] = rows[p * DEV : (p + 1) * DEV]
    aux[...] = jnp.zeros_like(aux)
    for r in range(CAP):
        aux[r, AUX * r : AUX * r + 1, :] = heat
        aux[r, AUX * r + 1 : AUX * r + 2, :] = coupling
        aux[r, AUX * r + 2 : AUX * r + AUX, :] = cells
    total = jnp.zeros((DEV, LANES), f32)
    for r in range(CAP):
        hi, lo = halves(aux[r])
        total = total + mm(picks[r], hi, NT) + mm(picks[r], lo, NT)
    out[pl.ds(CAP // 2, DEV, stride=FLUX_ROWS), :] = total


def payload(anchor, foot, coeff, walls, facade):
    return pl.pallas_call(
        payload_kernel,
        grid=(1,),
        in_specs=[
            whole((1, NB)),
            whole((FOOT, NB)),
            whole((6, NB)),
            pl.BlockSpec((6, 8, NB), lambda _: (0, 0, 0)),
            whole((LEV, NB)),
        ],
        out_specs=[whole((DEV * FLUX_ROWS, LANES)), whole((DEV, NB))],
        out_shape=[
            pltpu.HBM((DEV * FLUX_ROWS, LANES), f32),
            pltpu.HBM((DEV, NB), f32),
        ],
        scratch_shapes=[pltpu.VMEM((CAP, LANES, NB), f32)],
        compiler_params=params(),
        name="payload",
    )(anchor, foot, coeff, walls, facade)


def lane_slot():
    return lax.broadcasted_iota(jnp.int32, (8, LANES), 1)


def pack_row(blocks):
    lane = lane_slot()
    slot = lane % 16
    out = jnp.zeros((8, LANES), f32)
    for i, block in enumerate(blocks):
        here = lane // 16 == i
        west = here & (slot >= 4) & (slot < 8)
        east = here & (slot >= 8) & (slot < 12)
        out = jnp.where(west, pltpu.roll(block, (16 * i + 4) % LANES, 1), out)
        out = jnp.where(east, pltpu.roll(block, (16 * i + 12) % LANES, 1), out)
    return out


def emit_row(f, y, field, low, high, pack):
    dst = low if y < HALO else high
    dst[f, y % HALO, :LEV, :] = field
    row = pack_row([field[8 * i : 8 * i + 8] for i in range(8)])
    if y < HALO:
        pack[f, y] = row
    else:
        pack[f, y - HALO] = pack[f, y - HALO] + pltpu.roll(row, 8, 1)


def prep_kernel(courant_in, canopy, low, high, pack, coef, coef_strip, field, courant, sems):
    n = field.shape[0]
    loads = [pltpu.make_async_copy(canopy.at[NEAR + f], field.at[f], sems.at[f]) for f in range(n)]
    given = pltpu.make_async_copy(courant_in, courant, sems.at[n])
    given.start()
    for c in loads:
        c.start()
    given.wait()
    square = (LEV, LEV)
    diagonal = lax.broadcasted_iota(jnp.int32, square, 0) == lax.broadcasted_iota(jnp.int32, square, 1)

    def column(row):
        picked = jnp.where(diagonal, jnp.broadcast_to(courant[row : row + 1, :], square), 0.0)
        return jnp.broadcast_to(jnp.sum(picked, axis=1, keepdims=True), (LEV, LANES))

    cx, cy = column(0), column(1)
    values = (
        1.0 - jnp.abs(cx) - jnp.abs(cy) - (4.0 * kappa_rate + 2.0 * vertical_rate),
        jnp.maximum(cx, 0.0) + kappa_rate,
        kappa_rate - jnp.minimum(cx, 0.0),
        jnp.maximum(cy, 0.0) + kappa_rate,
        kappa_rate - jnp.minimum(cy, 0.0),
    )
    block = lane_slot() // 16
    for k, v in enumerate(values):
        coef[k] = v
        strip = v[0:8]
        for i in range(1, 8):
            strip = jnp.where(block == i, v[8 * i : 8 * i + 8], strip)
        coef_strip[k] = strip
    for f in range(n):
        loads[f].wait()
        for y in range(ROWS_Y):
            emit_row(f, y, field[f, pl.ds(y, LEV, stride=ROWS_Y), :], low, high, pack)


def half_shape(n):
    return jax.ShapeDtypeStruct((n, HALO, LEV + STRIP, LANES), f32)


def pack_shape(n):
    return jax.ShapeDtypeStruct((n, HALO, STRIP, LANES), f32)


def half_spec(n):
    return pl.BlockSpec((n, HALO, LEV, LANES), lambda i: (0, 0, 0, 0))


def prep(courant, canopy):
    n = canopy.shape[0] - NEAR
    return pl.pallas_call(
        prep_kernel,
        grid=(1,),
        in_specs=[REMOTE, REMOTE],
        out_specs=[
            half_spec(n),
            half_spec(n),
            whole((n, HALO, STRIP, LANES)),
            whole((5, LEV, LANES)),
            whole((5, STRIP, LANES)),
        ],
        out_shape=[
            half_shape(n),
            half_shape(n),
            pack_shape(n),
            pltpu.HBM((5, LEV, LANES), f32),
            pltpu.HBM((5, STRIP, LANES), f32),
        ],
        scratch_shapes=[
            pltpu.VMEM((n, LEV * ROWS_Y, LANES), f32),
            pltpu.VMEM((2, LEV), f32),
            pltpu.SemaphoreType.DMA((n + 1,)),
        ],
        compiler_params=params(),
        name="prep",
    )(courant, canopy)


def scatter_kernel(recv, canopy, counts_out, low, high, pack, counts, column_s, field_s, xt, near, sems):
    load = pltpu.make_async_copy(canopy.at[pl.ds(0, NEAR)], near, sems.at[0])
    load.start()
    aux = recv[pl.ds(CAP // 2, DEV, stride=FLUX_ROWS), :].T
    cell = aux.astype(jnp.int32)
    column_s[...] = cell & (LANES - 1)
    field_s[...] = lax.shift_left(jnp.ones_like(cell), lax.shift_right_logical(cell, jnp.full_like(cell, 5)) & 28)

    def group(g, carry):
        start = pl.multiple_of(g * 16, 16)
        x = lax.broadcasted_iota(jnp.int32, (16, LANES), 0) + start
        for r in range(CAP):
            packed = jnp.zeros((16, LANES), jnp.int32)
            for k in range(AUX * r + 2, AUX * r + AUX):
                here = jnp.broadcast_to(column_s[k : k + 1, :], (16, LANES)) == x
                packed = packed + jnp.where(here, jnp.broadcast_to(field_s[k : k + 1, :], (16, LANES)), 0)
            for y in range(ROWS_Y):
                n = lax.shift_right_logical(packed, jnp.full_like(packed, 4 * y)) & 15
                row = pl.multiple_of(y * LANES + start, 16)
                counts[pl.ds(row, 16), r * DEV : (r + 1) * DEV] = n.astype(f32).astype(bf16)
        return carry

    lax.fori_loop(0, LANES // 16, group, 0)
    save = pltpu.make_async_copy(counts, counts_out, sems.at[1])
    save.start()
    for p in range(CAP // 2):
        rows = recv[pl.ds(p, DEV, stride=FLUX_ROWS), :].T
        for odd in range(2):
            r = 2 * p + odd
            area = rows[LEV * odd : LEV * (odd + 1)]
            for q in range(2):
                hi, lo = halves(area * aux[AUX * r + q : AUX * r + q + 1, :])
                xt[q * LEV : (q + 1) * LEV, r * DEV : (r + 1) * DEV] = hi
                xt[DEV + q * LEV : DEV + (q + 1) * LEV, r * DEV : (r + 1) * DEV] = lo
    both = mm(xt[...], counts[...], NT)
    sums = both[:DEV] + both[DEV:]
    load.wait()
    for y in range(ROWS_Y):
        c = near[0, pl.ds(y, LEV, stride=ROWS_Y), :]
        p = sums[:LEV, y * LANES : (y + 1) * LANES]
        q = sums[LEV:, y * LANES : (y + 1) * LANES]
        emit_row(0, y, c + (source_rate / FOOT) * (p - q * c), low, high, pack)
        for f in range(1, NEAR):
            emit_row(f, y, near[f, pl.ds(y, LEV, stride=ROWS_Y), :], low, high, pack)
    save.wait()


def scatter(recv, canopy):
    return pl.pallas_call(
        scatter_kernel,
        grid=(1,),
        in_specs=[whole((DEV * FLUX_ROWS, LANES)), pl.BlockSpec(memory_space=pltpu.HBM)],
        out_specs=[
            REMOTE,
            half_spec(NEAR),
            half_spec(NEAR),
            whole((NEAR, HALO, STRIP, LANES)),
        ],
        out_shape=[
            pltpu.HBM((ROWS_Y * LANES, CAP * DEV), bf16),
            half_shape(NEAR),
            half_shape(NEAR),
            pack_shape(NEAR),
        ],
        scratch_shapes=[
            pltpu.VMEM((ROWS_Y * LANES, CAP * DEV), bf16),
            pltpu.VMEM((LANES, DEV), jnp.int32),
            pltpu.VMEM((LANES, DEV), jnp.int32),
            pltpu.VMEM((2 * DEV, CAP * DEV), bf16),
            pltpu.VMEM((NEAR, LEV * ROWS_Y, LANES), f32),
            pltpu.SemaphoreType.DMA((2,)),
        ],
        compiler_params=params(),
        name="scatter",
    )(recv, canopy)


def merge_kernel(pack, west, east, low_in, high_in, low, high):
    slot = lane_slot() % 16
    for f in range(pack.shape[0]):
        for y in range(ROWS_Y):
            w, own, e = west[f, y % HALO], pack[f, y % HALO], east[f, y % HALO]
            if y < HALO:
                w, e = pltpu.roll(w, LANES - 8, 1), pltpu.roll(e, 8, 1)
            else:
                w, own = pltpu.roll(w, LANES - 16, 1), pltpu.roll(own, LANES - 8, 1)
            dst = low if y < HALO else high
            dst[f, y % HALO] = jnp.where(slot < 4, w, jnp.where(slot < 12, own, e))


def merge(pack, west, east, low, high):
    n = pack.shape[0]
    pack_spec = whole((n, HALO, STRIP, LANES))
    strip_spec = pl.BlockSpec((n, HALO, STRIP, LANES), lambda i: (0, 0, LEV // STRIP, 0))
    anywhere = pl.BlockSpec(memory_space=pl.ANY)
    return pl.pallas_call(
        merge_kernel,
        grid=(1,),
        in_specs=[pack_spec, pack_spec, pack_spec, anywhere, anywhere],
        out_specs=[strip_spec, strip_spec],
        out_shape=[half_shape(n), half_shape(n)],
        input_output_aliases={3: 0, 4: 1},
        compiler_params=params(),
        name="merge",
    )(pack, west, east, low, high)


def shifts(axis):
    up = [(i, i + 1) for i in range(lax.axis_size(axis) - 1)]
    return up, [(j, i) for i, j in up]


def across_x(low, high, pack, beside=None):
    up, down = shifts("gx")
    west, east = lax.ppermute(pack, "gx", up), lax.ppermute(pack, "gx", down)
    done = None
    if beside is not None:
        done = beside()
        west, east, done = lax.optimization_barrier((west, east, done))
    low, high = merge(pack, west, east, low, high)
    return low, high, done


def across_y(low, high):
    up, down = shifts("gy")
    south, north = lax.ppermute(high, "gy", up), lax.ppermute(low, "gy", down)
    return south, low, high, north


def substeps(f, parts, coef, coef_strip, edge, buf, strips, ends, put):
    lane = lane_slot()
    sub = lax.broadcasted_iota(jnp.int32, (8, LANES), 0)
    slot = lane % 16
    first, last = lane == 0, lane == LANES - 1
    inside = jnp.where(slot < 4, edge[2], jnp.where(slot < 12, 1.0, edge[3]))
    total = ROWS_Y + 2 * HALO

    def keep(row, value):
        if row < HALO:
            return value * edge[0]
        if row >= HALO + ROWS_Y:
            return value * edge[1]
        return value

    table, sides, spread = ends
    starts = [0, 14, 26, 36]

    def strip(step, row):
        if step == 1:
            return parts[row // HALO][f, row % HALO, LEV : LEV + STRIP, :]
        return strips[(step + 1) % 2, row]

    for step in range(1, SUB + 1):
        c0, cw, ce, cs, cn = (coef_strip[k] for k in range(5))
        here, after = strip(step, step - 1), strip(step, step)
        for row in range(step, total - step):
            before, here, after = here, after, strip(step, row + 1)
            at = 8 * (starts[step - 1] + row - step)
            table[at : at + 8, :] = jnp.where(slot == 3, here, pltpu.roll(here, LANES - 10, 1))
            if step == SUB:
                continue
            down = pltpu.roll(here, 1, 0)
            below = jnp.where(sub == 0, jnp.where(lane < 16, here, pltpu.roll(down, 16, 1)), down)
            lift = pltpu.roll(here, 7, 0)
            above = jnp.where(sub == 7, jnp.where(lane >= LANES - 16, here, pltpu.roll(lift, LANES - 16, 1)), lift)
            value = (
                (c0 * here + cw * pltpu.roll(here, 1, 1))
                + (ce * pltpu.roll(here, LANES - 1, 1) + cs * before)
                + (cn * after + vertical_rate * (above + below))
            )
            strips[step % 2, row] = keep(row, value * inside)
    hi, lo = halves(table[...])
    sides[...] = mm(jnp.concatenate([hi, lo], axis=1), spread[...], NN)

    for step in range(1, SUB + 1):
        old, new = (step + 1) % 2, step % 2

        def main(row, start):
            if step == 1:
                return parts[row // HALO][f, row % HALO, start : start + 8, :]
            return buf[old, row, start : start + 8, :]

        for i in range(8):
            at = 8 * i
            c0, cw, ce, cs, cn = (coef[k, at : at + 8, :] for k in range(5))
            here, after = main(step - 1, at), main(step, at)
            for row in range(step, total - step):
                before, here, after = here, after, main(row + 1, at)
                if i == 0:
                    below = jnp.where(sub == 0, here, pltpu.roll(here, 1, 0))
                else:
                    below = pltpu.roll(jnp.where(sub == 7, main(row, at - 8), here), 1, 0)
                if i == 7:
                    above = jnp.where(sub == 7, here, pltpu.roll(here, 7, 0))
                else:
                    above = pltpu.roll(jnp.where(sub == 0, main(row, at + 8), here), 7, 0)
                line = 8 * (starts[step - 1] + row - step)
                side = sides[line : line + 8, i * LANES : (i + 1) * LANES]
                left = jnp.where(first, side, pltpu.roll(here, 1, 1))
                right = jnp.where(last, side, pltpu.roll(here, LANES - 1, 1))
                value = (
                    (c0 * here + cw * left)
                    + (ce * right + cs * before)
                    + (cn * after + vertical_rate * (above + below))
                )
                if step == SUB:
                    put(row - HALO, at, value)
                else:
                    buf[new, row, at : at + 8, :] = keep(row, value)


def fill_spread(spread):
    shape = (2 * LANES, 8 * LANES)
    src = lax.broadcasted_iota(jnp.int32, shape, 0) & (LANES - 1)
    col = lax.broadcasted_iota(jnp.int32, shape, 1)
    lane = col & (LANES - 1)
    base = lax.shift_right_logical(col, jnp.full_like(col, 7)) * 16
    hit = ((lane == 0) & (src == base + 3)) | ((lane == LANES - 1) & (src == base + 2))
    spread[...] = jnp.where(hit, 1.0, 0.0).astype(bf16)


def quarter_spec(n):
    return pl.BlockSpec((n, HALO, LEV + STRIP, LANES), lambda i: (i, 0, 0, 0))


STENCIL_SCRATCH = [
    pltpu.VMEM((2, ROWS_Y + 2 * HALO, LEV, LANES), f32),
    pltpu.VMEM((2, ROWS_Y + 2 * HALO, STRIP, LANES), f32),
    pltpu.VMEM((8 * 44, LANES), f32),
    pltpu.VMEM((8 * 44, 8 * LANES), f32),
    pltpu.VMEM((2 * LANES, 8 * LANES), bf16),
]


def coef_specs():
    return [
        whole((5, LEV, LANES)),
        whole((5, STRIP, LANES)),
        pl.BlockSpec(memory_space=pltpu.SMEM),
    ]


def fields_kernel(south, low, high, north, coef, coef_strip, edge, into, out, buf, strips, *ends):
    @pl.when(pl.program_id(0) == 0)
    def _():
        fill_spread(ends[2])

    def put(y, at, value):
        out[0, pl.ds(at * ROWS_Y + y, 8, stride=ROWS_Y), :] = value

    substeps(0, (south, low, high, north), coef, coef_strip, edge, buf, strips, ends, put)


def fields(parts, coefs, into):
    n = parts[0].shape[0]
    operands = [*parts, *coefs, into]
    return pl.pallas_call(
        fields_kernel,
        grid=(n,),
        in_specs=[quarter_spec(1) for _ in parts] + coef_specs() + [pl.BlockSpec(memory_space=pltpu.HBM)],
        out_specs=pl.BlockSpec((1, LEV * ROWS_Y, LANES), lambda i: (i + NEAR, 0, 0)),
        out_shape=pltpu.HBM(into.shape, f32),
        scratch_shapes=STENCIL_SCRATCH,
        input_output_aliases={len(operands) - 1: 0},
        compiler_params=params(),
        name="fields",
    )(*operands)


def gather_kernel(south, low, high, north, coef, coef_strip, edge, counts_in, fields_out, back, *scratch):
    buf, strips, *ends, table, counts, out, sems = scratch
    fill_spread(ends[2])
    fetch = pltpu.make_async_copy(counts_in, counts, sems.at[0])
    fetch.start()
    save = pltpu.make_async_copy(out, fields_out.at[pl.ds(0, NEAR)], sems.at[1])

    def field(f, carry):
        def put(y, at, value):
            out[f, pl.ds(at * ROWS_Y + y, 8, stride=ROWS_Y), :] = value

        substeps(f, (south, low, high, north), coef, coef_strip, edge, buf, strips, ends, put)
        return carry

    lax.fori_loop(0, NEAR, field, 0)
    save.start()
    for y in range(ROWS_Y):
        cols = slice(y * LANES, (y + 1) * LANES)
        for k in range(NEAR):
            hi, lo = halves(out[k, pl.ds(y, LEV, stride=ROWS_Y), :] * (1.0 / FOOT))
            table[k * LEV : (k + 1) * LEV, cols] = hi
            table[2 * LEV + k * LEV : 2 * LEV + (k + 1) * LEV, cols] = lo
    fetch.wait()
    both = mm(table[...], counts[...], NN)
    sums = both[: 2 * LEV] + both[2 * LEV :]
    for r in range(CAP):
        back[pl.ds(r, DEV, stride=CAP), :] = sums[:, r * DEV : (r + 1) * DEV].T
    save.wait()


def gather(parts, coefs, counts):
    return pl.pallas_call(
        gather_kernel,
        grid=(1,),
        in_specs=[quarter_spec(NEAR) for _ in parts] + coef_specs() + [REMOTE],
        out_specs=[
            REMOTE,
            whole((DEV * CAP, LANES)),
        ],
        out_shape=[
            pltpu.HBM((8, LEV * ROWS_Y, LANES), f32),
            pltpu.HBM((DEV * CAP, LANES), f32),
        ],
        scratch_shapes=STENCIL_SCRATCH
        + [
            pltpu.VMEM((4 * LEV, ROWS_Y * LANES), bf16),
            pltpu.VMEM((ROWS_Y * LANES, CAP * DEV), bf16),
            pltpu.VMEM((NEAR, LEV * ROWS_Y, LANES), f32),
            pltpu.SemaphoreType.DMA((2,)),
        ],
        compiler_params=params(),
        name="gather",
    )(*parts, *coefs, counts)


def walls_kernel(inverses, walls, package, product, column, inv_v, wall_v, out, a, b_hi, b_lo, inv_sem, sems, save_sems):
    surfaces, n, _ = wall_v.shape
    first = pltpu.make_async_copy(inverses, inv_v, inv_sem)
    first.start()

    def load(s):
        return pltpu.make_async_copy(walls.at[s], wall_v.at[s], sems.at[s])

    def save(s):
        return pltpu.make_async_copy(out.at[s], product.at[s], save_sems.at[s])

    for s in range(surfaces):
        load(s).start()
    first.wait()

    chosen = jnp.zeros((n, NB), f32)
    for p in range(PKG):
        inv = inv_v[p]
        hi, lo = halves(inv)
        a[:n, p * n : (p + 1) * n] = hi
        a[n:, p * n : (p + 1) * n] = lo
        chosen = jnp.where(package[...] == p, jnp.broadcast_to(inv[:, 0:1], (n, NB)), chosen)
    column[...] = chosen

    masks = [jnp.where(package[...] == p, 1.0, 0.0) for p in range(PKG)]

    def surface(s, carry):
        load(s).wait()
        w_hi, w_lo = halves(wall_v[s])
        for p in range(PKG):
            mine = jnp.broadcast_to(masks[p], (n, NB)).astype(bf16)
            b_hi[p * n : (p + 1) * n, :] = w_hi * mine
            b_lo[p * n : (p + 1) * n, :] = w_lo * mine
        both = mm(a[...], b_hi[...], NN)
        out[s] = both[:n] + both[n:] + mm(a[:n, :], b_lo[...], NN)
        save(s).start()
        return carry

    lax.fori_loop(0, surfaces, surface, 0)
    for s in range(surfaces):
        save(s).wait()


def walls_product(inverses, walls, package):
    s, n, _ = walls.shape
    return pl.pallas_call(
        walls_kernel,
        grid=(1,),
        in_specs=[REMOTE, REMOTE, whole((1, NB))],
        out_specs=[REMOTE, whole((n, NB))],
        out_shape=[pltpu.HBM((s, n, NB), f32), pltpu.HBM((n, NB), f32)],
        scratch_shapes=[
            pltpu.VMEM((PKG, n, n), f32),
            pltpu.VMEM((s, n, NB), f32),
            pltpu.VMEM((s, n, NB), f32),
            pltpu.VMEM((2 * n, PKG * n), bf16),
            pltpu.VMEM((PKG * n, NB), bf16),
            pltpu.VMEM((PKG * n, NB), bf16),
            pltpu.SemaphoreType.DMA,
            pltpu.SemaphoreType.DMA((s,)),
            pltpu.SemaphoreType.DMA((s,)),
        ],
        compiler_params=params(),
        name="walls",
    )(inverses, walls, package)


def final_kernel(recv, code_in, facade_in, coeff_in, walls, product, column_in, air_out, walls_out, *scratch):
    xt, code, facade, coeff, first, value, column, load_sems, sems = scratch
    surfaces = value.shape[0]
    pairs = (
        (code_in, code),
        (facade_in, facade),
        (coeff_in, coeff),
        (walls.at[:, pl.ds(0, 8), :], first),
        (product, value),
        (column_in, column),
    )
    loads = [pltpu.make_async_copy(src, dst, load_sems.at[i]) for i, (src, dst) in enumerate(pairs)]
    for c in loads:
        c.start()
    for r in range(CAP):
        hi, lo = halves(recv[pl.ds(r, DEV, stride=CAP), :].T)
        xt[:LANES, r * DEV : (r + 1) * DEV] = hi
        xt[LANES:, r * DEV : (r + 1) * DEV] = lo
    loads[0].wait()
    picks = []
    for r in range(CAP):
        picks.append(jnp.where(code[...] == float(r), 1.0, 0.0).astype(bf16))
    both = mm(xt[...], jnp.concatenate(picks, axis=0), NN)
    air = both[:LANES] + both[LANES:]
    air_out[...] = air
    for c in loads[1:]:
        c.wait()
    area = facade[...]
    temp = jnp.sum(area * air[:LEV], axis=0, keepdims=True) / jnp.sum(area, axis=0, keepdims=True)
    saves = []
    for s in range(surfaces):
        source = wall_gain * coeff[s : s + 1, :] * (temp - first[s, 0:1, :])
        value[s] = value[s] + column[...] * source
        saves.append(pltpu.make_async_copy(value.at[s], walls_out.at[s], sems.at[s]))
        saves[s].start()
    for c in saves:
        c.wait()


def final(recv, code, facade, coeff, walls, product, column):
    s, n, _ = walls.shape
    return pl.pallas_call(
        final_kernel,
        grid=(1,),
        in_specs=[
            whole((DEV * CAP, LANES)),
            REMOTE,
            REMOTE,
            REMOTE,
            REMOTE,
            REMOTE,
            REMOTE,
        ],
        out_specs=[whole((2 * LEV, NB)), REMOTE],
        out_shape=[
            jax.ShapeDtypeStruct((2 * LEV, NB), f32),
            pltpu.HBM((s, n, NB), f32),
        ],
        scratch_shapes=[
            pltpu.VMEM((2 * LANES, CAP * DEV), bf16),
            pltpu.VMEM((DEV, NB), f32),
            pltpu.VMEM((LEV, NB), f32),
            pltpu.VMEM((s, NB), f32),
            pltpu.VMEM((s, 8, NB), f32),
            pltpu.VMEM((s, n, NB), f32),
            pltpu.VMEM((n, NB), f32),
            pltpu.SemaphoreType.DMA((6,)),
            pltpu.SemaphoreType.DMA((s,)),
        ],
        compiler_params=params(),
        name="final",
    )(recv, code, facade, coeff, walls, product, column)


def transpose_all(x, rows):
    y = lax.all_to_all(
        x.reshape(DEV, 1, rows * LANES), ("gx", "gy"), split_axis=0, concat_axis=0, tiled=True
    )
    return y.reshape(DEV * rows, LANES)


def inside_edges():
    gx, gy = lax.axis_index("gx"), lax.axis_index("gy")
    side = jnp.arange(4, dtype=jnp.int32)
    place = jnp.where(side < 2, gy, gx)
    limit = jnp.where(side < 2, lax.axis_size("gy") - 1, lax.axis_size("gx") - 1)
    return jnp.where(side % 2 == 0, place > 0, place < limit).astype(f32)


def hbm(x):
    return pltpu.with_memory_space_constraint(x, pltpu.HBM)


def body(canopy, courant, walls, inverses, package, surf_coeff, facade_area, anchor, footprint):
    shape = canopy.shape
    canopy = canopy.reshape(shape[0], LEV * ROWS_Y, LANES)
    edge = inside_edges()
    send, code = payload(hbm(anchor.T), hbm(footprint.T), hbm(surf_coeff), hbm(walls), hbm(facade_area))
    recv = transpose_all(send, FLUX_ROWS)
    later, code = lax.optimization_barrier((canopy, code))
    low, high, pack, coef, coef_strip = prep(hbm(courant), hbm(later))
    coefs = (hbm(coef), hbm(coef_strip), edge)
    low, high, _ = across_x(low, high, pack)
    recv, low, high = lax.optimization_barrier((recv, low, high))
    up, down = shifts("gy")
    south = lax.ppermute(high, "gy", up)
    counts, near_low, near_high, pack = scatter(recv, hbm(canopy))
    near_low, near_high, _ = across_x(near_low, near_high, pack)
    near_low, near_high, low, walls_later = lax.optimization_barrier((near_low, near_high, low, walls))
    near = across_y(near_low, near_high)
    north = lax.ppermute(low, "gy", down)
    product, column = walls_product(hbm(inverses), hbm(walls_later), hbm(package[None, :]))
    near, south, product = lax.optimization_barrier((near, south, product))
    rest = (south, low, high, north)
    out, back = gather(near, coefs, hbm(counts))
    returned = transpose_all(back, CAP)
    out = fields(rest, coefs, out)
    air, walls_out = final(returned, hbm(code), hbm(facade_area), hbm(surf_coeff), hbm(walls), hbm(product), hbm(column))
    return out.reshape(shape), air.reshape(2, LEV, NB), walls_out


def solution(mesh):
    placed = (
        P(None, None, "gy", "gx"),
        P(),
        P(None, None, ("gx", "gy")),
        P(),
        P(("gx", "gy")),
        P(None, ("gx", "gy")),
        P(None, ("gx", "gy")),
        P(("gx", "gy"), None),
        P(("gx", "gy"), None),
    )
    return jax.shard_map(
        body,
        mesh=mesh,
        in_specs=placed,
        out_specs=(
            P(None, None, "gy", "gx"),
            P(None, None, ("gx", "gy")),
            P(None, None, ("gx", "gy")),
        ),
        check_vma=False,
    )
```
